128 devices in a mesh: prow: 4 (over y), pcol: 32 (over x, z, core).
Axes of the slice: x: 4, y: 4, z: 4, core: 2. Of those that a mesh axis runs over, the one named last changes fastest.
Arguments:
- matrix: float32 [16, 4, 128, 12, 32, 128], P(None, 'prow', None, None, 'pcol'), may hold values from -240 to 240, as said below
- pivots: int32 [2, 128], replicated, may hold values from 0 to 8191, as said below
Outputs:
- factored: float32 [16, 4, 128, 12, 32, 128], P(None, 'prow', None, None, 'pcol')
The draws below stay inside these ranges and needn't reach their ends.
Inputs may be any that keep to these rules, and one draw needn't show every extreme that they name: pivots[s] lists 128 distinct rows, each s * 128 or more; 8191 is among them, and row 0 is among those of pivots[0]. `matrix`: swapping by the listed rows leaves diagonal blocks whose factorization without further pivoting is well conditioned.
All inputs are finite; a program needn't handle non-finite values.
Results may differ from the reference program's by a relative error of at most 0.0001.
Values sent between devices are 32-bit elements; how exact they have to be, the bound alone decides.
A program may use at most 192 MiB of HBM per device.

```python
import jax
import jax.numpy as jnp
from jax import lax

NB = 128
LB = 16
CB = 12
M = 8192
COLS = 49152
N_PROW = 4
N_PCOL = 32


def spread_slots_drawn(picked, start_row, extent):
    block_rows = start_row + jnp.arange(extent, dtype=jnp.int32)
    in_block = jnp.any(picked[:, None] == block_rows[None, :], axis=0)
    vacated = picked >= start_row + extent
    displaced = jnp.logical_not(in_block)
    rank_vacated = jnp.cumsum(vacated.astype(jnp.int32)) - 1
    rank_displaced = jnp.cumsum(displaced.astype(jnp.int32)) - 1
    pairing = vacated[:, None] & displaced[None, :] & (rank_vacated[:, None] == rank_displaced[None, :])
    filler = jnp.sum(jnp.where(pairing, block_rows[None, :], 0), axis=1).astype(jnp.int32)
    return (vacated, filler)


def pivot_lists(key):
    list_key = jax.random.fold_in(key, 7)
    sections = []
    for section in range(2):
        section_key = jax.random.fold_in(list_key, section)
        if section == 0:
            chosen_rows = 1 + jax.random.choice(jax.random.fold_in(section_key, 1), M - 2, (NB - 2,), replace=False)
            complete = jnp.concatenate([chosen_rows.astype(jnp.int32), jnp.zeros((1,), jnp.int32), jnp.full((1,), M - 1, jnp.int32)])
        else:
            first_row = section * NB
            chosen_rows = first_row + jax.random.choice(jax.random.fold_in(section_key, 1), M - 1 - first_row, (NB - 1,), replace=False)
            complete = jnp.concatenate([chosen_rows.astype(jnp.int32), jnp.full((1,), M - 1, jnp.int32)])
        ordering = jax.random.permutation(jax.random.fold_in(section_key, 2), NB)
        sections.append(complete[ordering])
    return jnp.stack(sections).astype(jnp.int32)


def draw_pivots(key, part):
    return pivot_lists(key)


def draw_matrix(key, part):
    lists = pivot_lists(key)
    first_list = lists[0]
    second_list = lists[1]
    vacated, filler = spread_slots_drawn(first_list, 0, NB)
    source = jnp.arange(M, dtype=jnp.int32)
    source = source.at[:NB].set(first_list)
    source = source.at[jnp.where(vacated, first_list, M)].set(filler, mode='drop')
    second_rows = source[second_list]
    noise_key = jax.random.fold_in(key, 3)
    entries = jax.random.normal(noise_key, (M, COLS), jnp.float32)
    magnitude = 40.0 + 16.0 * jax.random.uniform(jax.random.fold_in(key, 4), (2, NB), jnp.float32)
    columns = jnp.arange(NB, dtype=jnp.int32)
    entries = entries.at[first_list, columns].set(magnitude[0])
    entries = entries.at[second_rows, NB + columns].set(magnitude[1])
    return entries.reshape(LB, N_PROW, NB, CB, N_PCOL, NB).astype(jnp.float32)


def setup_inputs(seed: int = 0) -> dict:
    streams_of = jax.random.split(jax.random.key(seed), 3)
    matrix = draw_matrix(jax.random.fold_in(streams_of[2], 71), 0)
    pivots = draw_pivots(jax.random.fold_in(streams_of[2], 71), 0)
    return {"matrix": matrix, "pivots": pivots}


HIGHEST_PREC = lax.Precision.HIGHEST


def lower_inverse(lower):
    extent = lower.shape[0]
    ident = jnp.eye(extent, dtype=jnp.float32)
    if extent <= 16:
        rows = [ident[0]]
        for index in range(1, extent):
            earlier = jnp.stack(rows)
            rows.append(ident[index] - jnp.sum(lower[index, :index][:, None] * earlier, axis=0))
        return jnp.stack(rows)
    half = extent // 2
    first = lower_inverse(lower[:half, :half])
    second = lower_inverse(lower[half:, half:])
    corner = -jnp.dot(second, jnp.dot(lower[half:, :half], first, precision=HIGHEST_PREC), precision=HIGHEST_PREC)
    top_half = jnp.concatenate([first, jnp.zeros((half, extent - half), jnp.float32)], 1)
    bottom_half = jnp.concatenate([corner, second], 1)
    return jnp.concatenate([top_half, bottom_half], 0)


def upper_inverse(upper):
    extent = upper.shape[0]
    ident = jnp.eye(extent, dtype=jnp.float32)
    if extent <= 16:
        rows = [ident[extent - 1] / upper[extent - 1, extent - 1]]
        for index in range(extent - 2, -1, -1):
            later = jnp.stack(rows[::-1])
            accum = ident[index] - jnp.sum(upper[index, index + 1:][:, None] * later, axis=0)
            rows.append(accum / upper[index, index])
        return jnp.stack(rows[::-1])
    half = extent // 2
    first = upper_inverse(upper[:half, :half])
    second = upper_inverse(upper[half:, half:])
    corner = -jnp.dot(first, jnp.dot(upper[:half, half:], second, precision=HIGHEST_PREC), precision=HIGHEST_PREC)
    top_half = jnp.concatenate([first, corner], 1)
    bottom_half = jnp.concatenate([jnp.zeros((extent - half, half), jnp.float32), second], 1)
    return jnp.concatenate([top_half, bottom_half], 0)


def factor_block(square):
    extent = square.shape[0]
    if extent <= 16:
        for pivot in range(extent - 1):
            column = square[pivot + 1:, pivot] / square[pivot, pivot]
            square = square.at[pivot + 1:, pivot].set(column)
            square = square.at[pivot + 1:, pivot + 1:].add(-column[:, None] * square[pivot, pivot + 1:][None, :])
        return square
    half = extent // 2
    upper_left = factor_block(square[:half, :half])
    upper_right = jnp.dot(lower_inverse(upper_left), square[:half, half:], precision=HIGHEST_PREC)
    lower_left = jnp.dot(square[half:, :half], upper_inverse(upper_left), precision=HIGHEST_PREC)
    schur = square[half:, half:] - jnp.dot(lower_left, upper_right, precision=HIGHEST_PREC)
    lower_right = factor_block(schur)
    top_half = jnp.concatenate([upper_left, upper_right], 1)
    bottom_half = jnp.concatenate([lower_left, lower_right], 1)
    return jnp.concatenate([top_half, bottom_half], 0)


def inverses(packed):
    return lower_inverse(packed), upper_inverse(packed)


def spread_slots(picked, start_row, extent):
    block_rows = start_row + jnp.arange(extent, dtype=jnp.int32)
    in_block = jnp.any(picked[:, None] == block_rows[None, :], axis=0)
    vacated = picked >= start_row + extent
    displaced = jnp.logical_not(in_block)
    rank_vacated = jnp.cumsum(vacated.astype(jnp.int32)) - 1
    rank_displaced = jnp.cumsum(displaced.astype(jnp.int32)) - 1
    pairing = vacated[:, None] & displaced[None, :] & (rank_vacated[:, None] == rank_displaced[None, :])
    filler = jnp.sum(jnp.where(pairing, block_rows[None, :], 0), axis=1).astype(jnp.int32)
    return vacated, filler


def reference(matrix, pivots):
    extent = NB
    whole = matrix.reshape(M, COLS)
    for section in range(2):
        start_row = section * extent
        finish = start_row + extent
        picked = pivots[section].astype(jnp.int32)
        vacated, filler = spread_slots(picked, start_row, extent)
        source = jnp.arange(M, dtype=jnp.int32)
        source = source.at[start_row:finish].set(picked)
        source = source.at[jnp.where(vacated, picked, M).astype(jnp.int32)].set(filler, mode="drop")
        whole = jnp.take(whole, source, axis=0)
        packed = factor_block(whole[start_row:finish, start_row:finish])
        lower_inv, upper_inv = inverses(packed)
        multiplier = jnp.dot(whole[finish:, start_row:finish], upper_inv, precision=HIGHEST_PREC)
        upper_rows = jnp.dot(lower_inv, whole[start_row:finish, finish:], precision=HIGHEST_PREC)
        trailing = whole[finish:, finish:] - jnp.dot(multiplier, upper_rows, precision=HIGHEST_PREC)
        whole = whole.at[start_row:finish, start_row:finish].set(packed)
        whole = whole.at[finish:, start_row:finish].set(multiplier)
        whole = whole.at[start_row:finish, finish:].set(upper_rows)
        whole = whole.at[finish:, finish:].set(trailing)
    return whole.reshape(matrix.shape)
```

```python
import jax
import jax.numpy as jnp
from jax import lax
from jax.experimental import pallas as pl
from jax.experimental.pallas import tpu as pltpu
from jax.sharding import PartitionSpec as P

NB = 128
F32 = jnp.float32
BF16 = jnp.bfloat16
MESH = pl.DeviceIdType.MESH
SLOTS_A = 96
SLOTS_D = 64
LOADS = 8
(
    OWNER, LOCAL, OVER, ARR_LOCAL, ARR_COUNT, OUT_LOCAL, OUT_SLOT, OUT_COUNT,
    IN_TARGET, IN_ROW, IN_LINE, IN_ORIGIN, IN_COUNT,
) = range(13)


def split(x):
    high = x.astype(BF16)
    return high, (x - high.astype(F32)).astype(BF16)


def dot(a, b):
    return jnp.dot(a, b, preferred_element_type=F32)


def dot3(a, b):
    ah, al = a
    bh, bl = b
    return dot(ah, bh) + (dot(ah, bl) + dot(al, bh))


def onehot_rows(onehot, x):
    high = x.astype(BF16)
    rest = x - high.astype(F32)
    mid = rest.astype(BF16)
    low = (rest - mid.astype(F32)).astype(BF16)
    return (dot(onehot, high) + dot(onehot, mid)) + dot(onehot, low)


def iota(shape, dim):
    return lax.broadcasted_iota(jnp.int32, shape, dim)


def eliminate(a_ref, xl_ref, xu_ref, t_ref, index, half):
    local = pl.multiple_of(index * 16, 16)
    start = pl.multiple_of(half * NB + local, 16)
    sub = iota((16, NB), 0)
    lane = iota((16, NB), 1)
    original = [a_ref[g, pl.ds(start, 16), :] for g in range(2)]
    rolled = pltpu.roll(original[half], lax.rem(NB - local, NB), axis=1)
    cols = [jnp.broadcast_to(rolled[:, j : j + 1], (16, NB)) for j in range(16)]
    upper = list(original[half:])
    jordan = list(original[half:])
    ident = jnp.where((lane == sub) | (lane == sub + 16), 1.0, 0.0).astype(F32)
    factors = jnp.zeros((16, NB), F32)
    scale = jnp.zeros((16, NB), F32)

    def pick(x, k):
        return jnp.broadcast_to(x[k : k + 1, :], (16, NB))

    for k in range(16):
        inverse = 1.0 / pick(cols[k], k)
        mult = cols[k] * inverse
        low = jnp.where(sub > k, mult, 0.0)
        both = jnp.where(sub != k, mult, 0.0)
        for j in range(k + 1, 16):
            cols[j] = cols[j] - both * pick(cols[j], k)
        upper = [x - low * pick(x, k) for x in upper]
        jordan = [x - both * pick(x, k) for x in jordan]
        mixed = jnp.where(lane < 16, low, both - low)
        ident = ident - mixed * pick(ident, k)
        factors = jnp.where((lane == local + k) & (sub > k), mult, factors)
        scale = jnp.where(sub == k, inverse, scale)

    in_block = (lane >= local) & (lane < local + 16)
    lower_of_block = in_block & (lane - local < sub)
    merged = jnp.where(lower_of_block, factors, jnp.where(lane < local, original[half], upper[0]))
    a_ref[half, pl.ds(start, 16), :] = merged
    if half == 0:
        a_ref[1, pl.ds(start, 16), :] = upper[1]
    left_inv = pltpu.roll(jnp.where(lane < 16, ident, 0.0), local, axis=1)
    right_inv = pltpu.roll(
        jnp.where((lane >= 16) & (lane < 32), ident * scale, 0.0), lax.rem(local + NB - 16, NB), axis=1
    )
    zero = jnp.zeros((16, NB), F32)
    xl_ref[half, pl.ds(start, 16), :] = left_inv
    xl_ref[1 - half, pl.ds(start, 16), :] = zero
    xu_ref[half, pl.ds(start, 16), :] = right_inv
    xu_ref[1 - half, pl.ds(start, 16), :] = zero

    t_ref[0, pl.ds(local, 16), :] = jnp.where(
        lane >= local + 16, jordan[0] * scale, jnp.where(in_block, right_inv, 0.0)
    )
    if half == 0:
        t_ref[1, pl.ds(local, 16), :] = jordan[1] * scale
    rows = 2 * NB - half * NB
    below = iota((rows, NB), 0) + half * NB >= start + 16
    wide_lane = iota((rows, NB), 1)
    block_lane = (wide_lane >= local) & (wide_lane < local + 16)
    panel = a_ref[half, half * NB :, :]
    panel_parts = split(panel)
    product = dot3(panel_parts, split(t_ref[0]))
    a_ref[half, half * NB :, :] = jnp.where(
        below, jnp.where(block_lane, product, panel - product), panel
    )
    if half == 0:
        other = a_ref[1]
        product = dot3(panel_parts, split(t_ref[1]))
        a_ref[1] = jnp.where(below, other - product, other)
    t_ref[0, pl.ds(local, 16), :] = zero
    if half == 0:
        t_ref[1, pl.ds(local, 16), :] = zero


def lu_core(a_ref, xl_ref, xu_ref, t_ref):
    t_ref[...] = jnp.zeros(t_ref.shape, F32)
    for half in range(2):
        def step(index, carry, half=half):
            eliminate(a_ref, xl_ref, xu_ref, t_ref, index, half)
            return carry
        lax.fori_loop(0, 8, step, 0)
    packed = jnp.concatenate([a_ref[0], a_ref[1]], 1)
    left = jnp.concatenate([xl_ref[0], xl_ref[1]], 1)
    right = jnp.concatenate([xu_ref[0], xu_ref[1]], 1)
    row = iota((256, 256), 0)
    col = iota((256, 256), 1)
    size = 16
    while size < 256:
        pair = row // (2 * size) == col // (2 * size)
        low_corner = pair & (row % (2 * size) >= size) & (col % (2 * size) < size)
        up_corner = pair & (row % (2 * size) < size) & (col % (2 * size) >= size)
        left_parts = split(left)
        right_parts = split(right)
        first = dot3(left_parts, split(jnp.where(low_corner, packed, 0.0)))
        second = dot3(right_parts, split(jnp.where(up_corner, packed, 0.0)))
        left = left - dot3(split(first), left_parts)
        right = right - dot3(split(second), right_parts)
        size *= 2
    return packed, left, right


def lu_kernel(arr_ref, slot_ref, packed_ref, linv_ref, uinv_ref, a_ref, xl_ref, xu_ref, t_ref):
    count = arr_ref.shape[1]
    slot = slot_ref[:, :1]
    onehot = jnp.where(iota((256, count), 1) == slot, 1.0, 0.0).astype(BF16)
    for half in range(2):
        a_ref[half] = onehot_rows(onehot, arr_ref[half])
    packed, left, right = lu_core(a_ref, xl_ref, xu_ref, t_ref)
    packed_ref[...] = packed
    linv_ref[...] = left
    uinv_ref[...] = right


def lu_call(arr, slot_col):
    square = jax.ShapeDtypeStruct((256, 256), F32)
    whole = pl.BlockSpec((256, 256), lambda i: (0, 0))
    return pl.pallas_call(
        lu_kernel,
        grid=(1,),
        in_specs=[
            pl.BlockSpec((2, 4 * SLOTS_A, NB), lambda i: (0, 0, 0)),
            pl.BlockSpec((256, NB), lambda i: (0, 0)),
        ],
        out_specs=[whole] * 3,
        out_shape=[square] * 3,
        scratch_shapes=[pltpu.VMEM((2, 256, 128), F32)] * 3 + [pltpu.VMEM((2, 128, 128), F32)],
        compiler_params=pltpu.CompilerParams(vmem_limit_bytes=32 * 2**20),
        name="factor",
    )(arr, slot_col)


def index_kernel(piv_ref, idx_ref, slot_ref):
    lane = iota((NB, NB), 1).astype(F32)
    sub = iota((NB, NB), 0).astype(F32)

    def rows(x):
        return jnp.broadcast_to(x, (NB, NB))

    def lanes_sum(cond, value=1.0):
        return rows(jnp.sum(jnp.where(cond, value, 0.0), axis=1, keepdims=True))

    def subs_sum(cond, value=1.0):
        return rows(jnp.sum(jnp.where(cond, value, 0.0), axis=0, keepdims=True))

    given = piv_ref[...].astype(F32)
    row = [rows(given[s : s + 1, :]) for s in range(2)]
    col = [x.T for x in row]
    fill_row, fill_col = [], []
    for s in range(2):
        start = float(s * NB)
        listed_row = subs_sum(col[s] == lane + start)
        listed_col = lanes_sum(row[s] == sub + start)
        rank_vacated = lanes_sum((lane <= sub) & (row[s] >= start + NB))
        rank_displaced = subs_sum((sub <= lane) & (listed_col == 0.0))
        pairing = (col[s] >= start + NB) & (listed_row == 0.0) & (rank_vacated == rank_displaced)
        filler = lanes_sum(pairing, lane + start)
        fill_col.append(filler)
        fill_row.append(filler.T)
    again = col[1] == row[0]
    source_col = jnp.where(lanes_sum(again) > 0.0, lanes_sum(again, fill_row[0]), col[1])
    moved = fill_col[1] == row[0]
    second_col = jnp.where(lanes_sum(moved) > 0.0, lanes_sum(moved, fill_row[0]), fill_col[1])

    def whole(x):
        return x.astype(jnp.int32)

    def place(value):
        number = whole(value)
        return (number >> 7) & 3, (number >> 9) * NB + (number & (NB - 1))

    def ranks(keys):
        keys_row = [k.astype(F32) for k in keys]
        keys_col = [k.T for k in keys_row]
        first = subs_sum((keys_col[0] == keys_row[0]) & (sub < lane))
        second = subs_sum((keys_col[1] == keys_row[1]) & (sub < lane)) + subs_sum(
            keys_col[0] == keys_row[1]
        )
        return [whole(first), whole(second)]

    sources = [row[0], source_col.T]
    owners, locals_ = zip(*[place(x) for x in sources])
    rank_arr = ranks(owners)
    slots = [o * SLOTS_A + r for o, r in zip(owners, rank_arr)]
    valid = [(row[0] >= 2.0 * NB) & (subs_sum(again) == 0.0), row[1] >= 2.0 * NB]
    origins = [whole(fill_row[0]), whole(second_col.T)]
    dests, targets = zip(*[place(x) for x in row])
    halves = [x >> 7 for x in origins]
    keys = [jnp.where(v, h * 4 + d, 9) for v, h, d in zip(valid, halves, dests)]
    rank_disp = ranks(keys)
    zero = jnp.zeros((NB, NB), jnp.int32)
    over = zero
    for g in range(2):
        over = over + whole(rows(jnp.sum(jnp.where(rank_arr[g] >= SLOTS_A, 1.0, 0.0), axis=1, keepdims=True)))
        bad = valid[g] & (rank_disp[g] >= SLOTS_D)
        over = over + whole(rows(jnp.sum(jnp.where(bad, 1.0, 0.0), axis=1, keepdims=True)))
    me = lax.axis_index("prow")

    def compact(chosen, values):
        chosen = [jnp.where(c, 1.0, 0.0) for c in chosen]
        chosen_col = [c.T for c in chosen]
        first = subs_sum((chosen_col[0] > 0.0) & (sub < lane))
        total = subs_sum(chosen_col[0] > 0.0)
        second = subs_sum((chosen_col[1] > 0.0) & (sub < lane)) + total
        order = [jnp.where(c > 0.0, r, -1.0).T for c, r in zip(chosen, (first, second))]
        packed = []
        for value in values:
            value_col = [v.astype(F32).T for v in value]
            packed.append(
                [
                    whole(sum(subs_sum(o == lane + g * NB, v) for o, v in zip(order, value_col)))
                    for g in range(2)
                ]
            )
        count = whole(total + subs_sum(chosen_col[1] > 0.0))
        return packed, [count, count]

    (arr_local,), arr_count = compact([o == me for o in owners], [locals_])
    (out_local, out_slot), out_count = compact(
        [v & (h == me) for v, h in zip(valid, halves)],
        [
            [x & (NB - 1) for x in origins],
            [d * SLOTS_D + r for d, r in zip(dests, rank_disp)],
        ],
    )
    (in_target, in_row, in_line, in_origin), in_count = compact(
        [v & (d == me) for v, d in zip(valid, dests)],
        [
            targets,
            [h * NB + r for h, r in zip(halves, rank_disp)],
            [h * SLOTS_D + r for h, r in zip(halves, rank_disp)],
            origins,
        ],
    )
    fields = [
        owners, locals_, [over, over], arr_local, arr_count, out_local, out_slot, out_count,
        in_target, in_row, in_line, in_origin, in_count,
    ]
    for number, field in enumerate(fields):
        for g in range(2):
            idx_ref[number : number + 1, g * NB : (g + 1) * NB] = field[g][0:1, :]
    for number in range(len(fields), 16):
        idx_ref[number : number + 1, :] = jnp.zeros((1, 2 * NB), jnp.int32)
    for g in range(2):
        slot_ref[g * NB : (g + 1) * NB, :] = whole(slots[g].astype(F32).T)


def index_call(pivots):
    return pl.pallas_call(
        index_kernel,
        out_shape=[
            jax.ShapeDtypeStruct((16, 2 * NB), jnp.int32),
            jax.ShapeDtypeStruct((2 * NB, NB), jnp.int32),
        ],
        name="indices",
    )(pivots)


def gather_kernel(idx_ref, x_ref, arr_ref, disp_ref, arr_line_ref, disp_line_ref, raw_ref, whole, sems):
    me = lax.axis_index("prow")
    lines = whole.shape[0] // (16 * NB)
    part = whole.shape[0] // LOADS
    loads = []
    for number in range(LOADS):
        here = pl.ds(number * part, part)
        loads.append(pltpu.make_async_copy(x_ref.at[here], whole.at[here], sems.at[number]))
        loads[-1].start()
    arr_ref[...] = jnp.zeros(arr_ref.shape, F32)
    for load in loads:
        load.wait()

    def arriving(j, carry):
        arr_ref[pl.ds(j * lines, lines), :] = whole[pl.ds(idx_ref[ARR_LOCAL, j] * lines, lines), :]
        return carry

    def displaced(t, carry):
        disp_ref[pl.ds(idx_ref[OUT_SLOT, t] * lines, lines), :] = whole[
            pl.ds(idx_ref[OUT_LOCAL, t] * lines, lines), :
        ]
        return carry

    lax.fori_loop(0, idx_ref[ARR_COUNT, 0], arriving, 0)
    lax.fori_loop(0, idx_ref[OUT_COUNT, 0], displaced, 0)
    arr_line_ref[...] = arr_ref[pl.ds(0, SLOTS_A, lines), :]
    disp_line_ref[...] = disp_ref[pl.ds(0, 4 * SLOTS_D, lines), :]
    raw_ref[...] = whole[pl.ds(0, 16 * NB, lines), :]


ANY = pl.BlockSpec(memory_space=pl.ANY)


def gather_call(idx, x, lines):
    sizes = [SLOTS_A * lines, 4 * SLOTS_D * lines, SLOTS_A, 4 * SLOTS_D, 16 * NB]
    vmem = pl.BlockSpec(memory_space=pltpu.VMEM)
    return pl.pallas_call(
        gather_kernel,
        in_specs=[pl.BlockSpec(memory_space=pltpu.SMEM), ANY],
        out_specs=[vmem] * 5,
        out_shape=[jax.ShapeDtypeStruct((size, NB), F32) for size in sizes],
        scratch_shapes=[pltpu.VMEM(x.shape, F32), pltpu.SemaphoreType.DMA((LOADS,))],
        compiler_params=pltpu.CompilerParams(vmem_limit_bytes=40 * 2**20),
        name="gather",
    )(idx, x)


DISP_LINES = 4 * SLOTS_A
RAW_LINES = DISP_LINES + 2 * NB
TREE_BLOCKS = 5


def rows8(start, size):
    return pl.ds(pl.multiple_of(start, 8), size)


def exchange_kernel(
    arr_ref, disp_ref, arr_line_ref, disp_line_ref, raw_ref, recv_arr, recv_disp, panel, relay,
    local_sem, y_send, y_recv, p_send, p_recv, t_send, t_recv, s_send, s_recv,
):
    p = lax.axis_index("prow")
    q = lax.axis_index("pcol")
    cx, cz, core = q // 8, (q // 2) % 4, q % 2
    root = q < 2

    def column(ix, iz, icore):
        return ((ix + 4) % 4 * 4 + (iz + 4) % 4) * 2 + icore

    up, down, across = ((p + 1) % 4, q), ((p + 3) % 4, q), ((p + 2) % 4, q)
    sibling = (p, column(cx, cz, 1 - core))
    near = [
        up, down, across, sibling,
        (p, column(cx + 1, cz, core)), (p, column(cx + 3, cz, core)),
        (p, column(cx, cz + 1, core)), (p, column(cx, cz + 3, core)),
    ]
    barrier = pltpu.get_barrier_semaphore()
    for other in near:
        pl.semaphore_signal(barrier, inc=1, device_id=other, device_id_type=MESH)
    pl.semaphore_wait(barrier, len(near))

    def remote(src, dst, send, recv, device):
        return pltpu.make_async_remote_copy(
            src_ref=src, dst_ref=dst, send_sem=send, recv_sem=recv, device_id=device, device_id_type=MESH
        )

    def arr_lines(owner):
        return panel.at[core, rows8(owner * SLOTS_A, SLOTS_A)]

    def disp_lines(half):
        return panel.at[core, rows8(DISP_LINES + half * SLOTS_D, SLOTS_D)]

    def disp_for(owner):
        return disp_line_ref.at[rows8(owner * SLOTS_D, SLOTS_D)]

    peers = [up, down, across]
    own_raw = pltpu.make_async_copy(raw_ref, panel.at[core, pl.ds(RAW_LINES, 16 * NB)], local_sem.at[0])
    own_arr = pltpu.make_async_copy(arr_line_ref, arr_lines(p), local_sem.at[1])
    own_disp = pltpu.make_async_copy(disp_for(p), disp_lines(p % 2), local_sem.at[2])
    arr_panel = [
        remote(arr_line_ref, arr_lines(p), p_send.at[i], p_recv.at[i], peers[i]) for i in range(3)
    ]
    disp_panel = [
        remote(disp_for(peers[i][0]), disp_lines(p % 2), p_send.at[3 + i], p_recv.at[3 + p % 2], peers[i])
        for i in range(3)
    ]

    @pl.when(root)
    def _():
        for copy in arr_panel:
            copy.start()

        @pl.when(p < 2)
        def _():
            for copy in disp_panel:
                copy.start()
            own_disp.start()

        own_arr.start()
        own_raw.start()

    arr_size, disp_size = arr_ref.shape[0], disp_ref.shape[0] // 4
    half_size = arr_size // 2
    low, high = pl.ds(0, half_size), pl.ds(half_size, half_size)

    def arr_rows(owner, part):
        return recv_arr.at[rows8(owner * arr_size + part.start, part.size)]

    def moved_to(owner):
        return disp_ref.at[rows8(owner * disp_size, disp_size)]

    def moved(half):
        return recv_disp.at[rows8(half * (recv_disp.shape[0] // 2), disp_size)]

    own_rows = pltpu.make_async_copy(arr_ref, recv_arr.at[rows8(p * arr_size, arr_size)], local_sem.at[3])
    own_moved = pltpu.make_async_copy(moved_to(p), moved(p % 2), local_sem.at[4])
    bulk = [
        remote(arr_ref.at[low], arr_rows(p, low), y_send.at[0], y_recv.at[0], up),
        remote(arr_ref.at[high], arr_rows(p, high), y_send.at[1], y_recv.at[1], down),
        remote(arr_ref.at[high], arr_rows(p, high), y_send.at[2], y_recv.at[2], up),
        remote(arr_ref.at[low], arr_rows(p, low), y_send.at[3], y_recv.at[3], down),
    ]
    for copy in bulk:
        copy.start()
    own_rows.start()

    half = p % 2
    to_up = remote(moved_to(up[0]), moved(half), y_send.at[4], y_recv.at[4 + half], up)
    to_down = remote(moved_to(down[0]), moved(half), y_send.at[5], y_recv.at[4 + half], down)
    via = [
        remote(moved_to(2), relay, y_send.at[6], y_recv.at[6], down),
        remote(moved_to(3), relay, y_send.at[6], y_recv.at[6], up),
    ]

    @pl.when(p < 2)
    def _():
        to_up.start()
        to_down.start()
        own_moved.start()

    for number in range(2):
        @pl.when(p == number)
        def _(number=number):
            via[number].start()

    forward = [
        remote(arr_rows(down[0], low), arr_rows(down[0], low), y_send.at[7], y_recv.at[7], up),
        remote(arr_rows(up[0], high), arr_rows(up[0], high), y_send.at[8], y_recv.at[8], down),
    ]

    def block(which, stream, k):
        line = jnp.where(k == 0, stream * NB, RAW_LINES + (stream * (TREE_BLOCKS - 1) + k - 1) * NB)
        return panel.at[which, pl.ds(pl.multiple_of(line, NB), NB)]

    def along(stream):
        sign = 1 if stream % 2 == 0 else 3
        return sign, (cx * sign) % 4, (cz * sign) % 4

    def tree(stream, k):
        sign, ax, az = along(stream)
        next_x = (p, column(cx + sign, cz, core))
        next_z = (p, column(cx, cz + sign, core))
        first, second = (ax, az) if stream < 2 else (az, ax)
        to_first, to_second = (next_x, next_z) if stream < 2 else (next_z, next_x)
        number = stream * TREE_BLOCKS + k
        ref = block(core, stream, k)
        return (
            (second == 0) & (first < 3),
            remote(ref, ref, t_send.at[0, number], t_recv.at[number], to_first),
            second < 3,
            remote(ref, ref, t_send.at[1, number], t_recv.at[number], to_second),
            remote(ref, ref, s_send.at[number], s_recv.at[number], sibling),
        )

    def pass_on(stream, step):
        _, ax, az = along(stream)
        depth = ax + az
        k = step - depth

        @pl.when((k >= 0) & (k < TREE_BLOCKS))
        def _():
            go_first, send_first, go_second, send_second, send_sibling = tree(stream, k)

            @pl.when(depth > 0)
            def _():
                send_first.wait_recv()

            @pl.when(go_first)
            def _():
                send_first.start()

            @pl.when(go_second)
            def _():
                send_second.start()

            send_sibling.start()

    @pl.when(root)
    def _():
        own_arr.wait()
        for copy in arr_panel:
            copy.wait_recv()
        for source in range(2):
            @pl.when(p == source)
            def _():
                own_disp.wait()

            @pl.when(p != source)
            def _(source=source):
                remote(disp_for(0), disp_lines(source), p_send.at[3], p_recv.at[3 + source], up).wait_recv()
        own_raw.wait()

    def tree_step(step, carry):
        for stream in range(4):
            pass_on(stream, step)
        return carry

    lax.fori_loop(0, 6, tree_step, 0)
    bulk[0].wait_recv()
    forward[0].start()
    bulk[1].wait_recv()
    forward[1].start()
    lax.fori_loop(6, 6 + TREE_BLOCKS, tree_step, 0)
    for number in range(2):
        @pl.when(p == 3 - number)
        def _(number=number):
            target = (2, q) if number == 0 else (3, q)
            remote(relay, relay, y_send.at[6], y_recv.at[6], target).wait_recv()
            onward = remote(relay, moved(number), y_send.at[9], y_recv.at[4 + number], target)
            onward.start()
            onward.wait_send()
    bulk[2].wait_recv()
    bulk[3].wait_recv()
    for copy in forward:
        copy.wait_recv()
    own_rows.wait()
    for source in range(2):
        @pl.when(p == source)
        def _():
            own_moved.wait()

        @pl.when(p != source)
        def _(source=source):
            remote(moved_to(0), moved(source), y_send.at[4], y_recv.at[4 + source], up).wait_recv()
    for copy in bulk + forward:
        copy.wait_send()

    @pl.when(p < 2)
    def _():
        to_up.wait_send()
        to_down.wait_send()
        via[0].wait_send()

    def finish(k, carry):
        for stream in range(4):
            go_first, send_first, go_second, send_second, send_sibling = tree(stream, k)

            @pl.when(go_first)
            def _():
                send_first.wait_send()

            @pl.when(go_second)
            def _():
                send_second.wait_send()

            send_sibling.wait_send()
            send_sibling.wait_recv()
        return carry

    lax.fori_loop(0, TREE_BLOCKS, finish, 0)

    @pl.when(root)
    def _():
        for copy in arr_panel:
            copy.wait_send()

        @pl.when(p < 2)
        def _():
            for copy in disp_panel:
                copy.wait_send()


def exchange_call(operands, lines):
    dma = pltpu.SemaphoreType.DMA
    sizes = [(4 * SLOTS_A * lines,), (2 * NB * lines,), (2, RAW_LINES + 16 * NB), (SLOTS_D * lines,)]
    return pl.pallas_call(
        exchange_kernel,
        in_specs=[pl.BlockSpec(memory_space=pltpu.VMEM)] * 5,
        out_specs=[ANY] * 4,
        out_shape=[jax.ShapeDtypeStruct(size + (NB,), F32) for size in sizes],
        scratch_shapes=[
            dma((5,)), dma((10,)), dma((9,)), dma((6,)), dma((5,)), dma((2, 20)), dma((20,)), dma((20,)), dma((20,)),
        ],
        compiler_params=pltpu.CompilerParams(collective_id=0, has_side_effects=True),
        name="exchange",
    )(*operands)


STEP_ROWS = 256


def update_kernel(
    idx_ref, x_ref, panel_ref, disp_ref, arr_ref, slot_ref, packed_ref, linv_ref, uinv_ref, o_ref,
    whole, pan, stacked, u_ref, x_sem, pan_sem,
):
    p = lax.axis_index("prow")
    q = lax.axis_index("pcol")
    step = pl.program_id(0)
    lines = whole.shape[0] // (16 * NB)

    @pl.when(step == 0)
    def _():
        load = pltpu.make_async_copy(x_ref, whole, x_sem)
        load.start()
        load_panel = pltpu.make_async_copy(panel_ref, pan, pan_sem)
        load_panel.start()
        high, low = split(linv_ref[...])
        slot = slot_ref[:, :1]
        onehot = jnp.where(iota((2 * NB, 4 * SLOTS_A), 1) == slot, 1.0, 0.0).astype(BF16)
        left = (dot(high, onehot).astype(BF16), dot(low, onehot).astype(BF16))
        for c in range(lines):
            rows = arr_ref[pl.ds(c, 4 * SLOTS_A, lines), :]
            value = dot3(left, split(rows))
            here = slice(c * NB, (c + 1) * NB)
            u_ref[:, here] = value
            upper, rest = split(value)
            stacked[0 : 2 * NB, here] = upper
            stacked[2 * NB : 4 * NB, here] = rest
            stacked[4 * NB : 6 * NB, here] = upper
        load_panel.wait()
        load.wait()

        def patch(t, carry):
            target = idx_ref[IN_TARGET, t]
            line = idx_ref[IN_LINE, t] + DISP_LINES
            for half in range(2):
                pan[half, pl.ds(RAW_LINES + target, 1), :] = pan[half, pl.ds(line, 1), :]
            source = idx_ref[IN_ROW, t] * lines
            whole[pl.ds(target * lines, lines), :] = disp_ref[pl.ds(source, lines), :]
            return carry

        lax.fori_loop(0, idx_ref[IN_COUNT, 0], patch, 0)

    here = pl.ds(pl.multiple_of(RAW_LINES + step * STEP_ROWS, NB), STEP_ROWS)
    rows = jnp.concatenate([pan[0, here, :], pan[1, here, :]], 1)
    mult = dot3(split(rows), split(uinv_ref[...]))
    high, low = split(mult)
    left = jnp.concatenate([high, high, low], 1)
    base = step * (STEP_ROWS * lines)
    for c in range(0, lines, 2):
        product = dot(left, stacked[:, c * NB : (c + 2) * NB])
        for k in range(2):
            current = whole[pl.ds(base + c + k, STEP_ROWS, lines), :]
            o_ref[pl.ds(c + k, STEP_ROWS, lines), :] = current - product[:, k * NB : (k + 1) * NB]

    for half in range(2):
        @pl.when(q == half)
        def _(half=half):
            o_ref[pl.ds(0, STEP_ROWS, lines), :] = mult[:, half * NB : (half + 1) * NB]

    for half in range(2):
        @pl.when((p == half) & (step == 0))
        def _(half=half):
            top = slice(half * NB, (half + 1) * NB)
            for c in range(lines):
                value = u_ref[top, c * NB : (c + 1) * NB]
                if c == 0:
                    value = jnp.where(q == 0, packed_ref[top, :NB], jnp.where(q == 1, packed_ref[top, NB:], value))
                o_ref[pl.ds(c, NB, lines), :] = value


def update_call(idx, x, panel, disp, arr, slot, packed, linv, uinv, lines):
    vmem = pl.BlockSpec(memory_space=pltpu.VMEM)
    return pl.pallas_call(
        update_kernel,
        grid=(16 * NB // STEP_ROWS,),
        in_specs=[pl.BlockSpec(memory_space=pltpu.SMEM), ANY, ANY] + [vmem] * 6,
        out_specs=pl.BlockSpec((STEP_ROWS * lines, NB), lambda i: (i, 0)),
        out_shape=jax.ShapeDtypeStruct((16 * NB * lines, NB), F32),
        scratch_shapes=[
            pltpu.VMEM((16 * NB * lines, NB), F32),
            pltpu.VMEM((2, RAW_LINES + 16 * NB, NB), F32),
            pltpu.VMEM((6 * NB, NB * lines), BF16),
            pltpu.VMEM((2 * NB, NB * lines), F32),
            pltpu.SemaphoreType.DMA,
            pltpu.SemaphoreType.DMA,
        ],
        compiler_params=pltpu.CompilerParams(vmem_limit_bytes=48 * 2**20),
        name="update",
    )(idx, x, panel, disp, arr, slot, packed, linv, uinv)


def shards(matrix, pivots):
    lines = matrix.shape[3]
    rows = matrix.shape[0] * NB
    p = lax.axis_index("prow")
    q = lax.axis_index("pcol")
    x = matrix.reshape(rows * lines, NB)
    idx, slot = index_call(pivots)

    def fits(x, idx, slot):
        recv_arr, recv_disp, panel, _ = exchange_call(gather_call(idx, x, lines), lines)
        return recv_arr, recv_disp, panel, idx, slot

    def general(x, idx, slot):
        x = x.reshape(rows, lines, NB)
        chosen = jnp.where((idx[OWNER] == p)[:, None, None], jnp.take(x, idx[LOCAL], axis=0), 0.0)
        top = jnp.concatenate([jnp.where(p == s, x[:NB], 0.0) for s in range(2)])
        chosen, top = lax.psum((chosen, top), "prow")
        chosen = jnp.pad(chosen, ((0, 4 * SLOTS_A - 2 * NB), (0, 0), (0, 0)))
        own = jnp.concatenate([chosen[:, 0], top[:, 0], x[:, 0]])
        panel = lax.psum(jnp.stack([jnp.where(q == s, own, 0.0) for s in range(2)]), "pcol")
        order = jnp.arange(2 * NB, dtype=jnp.int32)
        idx = idx.at[IN_ROW].set(idx[IN_ORIGIN]).at[IN_LINE].set(idx[IN_ORIGIN])
        slot = jnp.broadcast_to(order[:, None], slot.shape)
        return chosen.reshape(-1, NB), top.reshape(-1, NB), panel, idx, slot

    arr, disp, panel, idx, slot = lax.cond(idx[OVER, 0] == 0, fits, general, x, idx, slot)
    packed, linv, uinv = lu_call(panel, slot)
    out = update_call(idx, x, panel, disp, arr, slot, packed, linv, uinv, lines)
    return out.reshape(matrix.shape)


def solution(mesh):
    placed = (P(None, "prow", None, None, "pcol", None), P())
    return jax.shard_map(
        shards,
        mesh=mesh,
        in_specs=placed,
        out_specs=P(None, "prow", None, None, "pcol", None),
        check_vma=False,
    )
```

```python
import jax
import jax.numpy as jnp
from jax import lax
from jax.experimental import pallas as pl
from jax.experimental.pallas import tpu as pltpu
from jax.sharding import PartitionSpec as P

NB = 128
F32 = jnp.float32
BF16 = jnp.bfloat16
MESH = pl.DeviceIdType.MESH
SLOTS_A = 96
SLOTS_D = 64
LOADS = 16
PIECE = NB + 16
(
    OWNER, LOCAL, OVER, ARR_LOCAL, OUT_LOCAL, IN_TARGET, IN_ROW, IN_LINE, IN_ORIGIN, IN_COUNT,
) = range(10)


def split(x):
    high = x.astype(BF16)
    return high, (x - high.astype(F32)).astype(BF16)


def dot(a, b):
    return jnp.dot(a, b, preferred_element_type=F32)


def dot3(a, b):
    ah, al = a
    bh, bl = b
    return dot(ah, bh) + (dot(ah, bl) + dot(al, bh))


def onehot_rows(onehot, x):
    high = x.astype(BF16)
    rest = x - high.astype(F32)
    mid = rest.astype(BF16)
    low = (rest - mid.astype(F32)).astype(BF16)
    return (dot(onehot, high) + dot(onehot, mid)) + dot(onehot, low)


def iota(shape, dim):
    return lax.broadcasted_iota(jnp.int32, shape, dim)


def eliminate(a_ref, xl_ref, xu_ref, t_ref, index, half):
    local = pl.multiple_of(index * 16, 16)
    start = pl.multiple_of(half * NB + local, 16)
    sub = iota((16, NB), 0)
    lane = iota((16, NB), 1)
    original = [a_ref[g, pl.ds(start, 16), :] for g in range(2)]
    rolled = pltpu.roll(original[half], lax.rem(NB - local, NB), axis=1)
    cols = [jnp.broadcast_to(rolled[:, j : j + 1], (16, NB)) for j in range(16)]
    upper = list(original[half:])
    jordan = list(original[half:])
    ident = jnp.where((lane == sub) | (lane == sub + 16), 1.0, 0.0).astype(F32)
    factors = jnp.zeros((16, NB), F32)
    scale = jnp.zeros((16, NB), F32)

    def pick(x, k):
        return jnp.broadcast_to(x[k : k + 1, :], (16, NB))

    for k in range(16):
        inverse = 1.0 / pick(cols[k], k)
        mult = cols[k] * inverse
        low = jnp.where(sub > k, mult, 0.0)
        both = jnp.where(sub != k, mult, 0.0)
        for j in range(k + 1, 16):
            cols[j] = cols[j] - both * pick(cols[j], k)
        upper = [x - low * pick(x, k) for x in upper]
        jordan = [x - both * pick(x, k) for x in jordan]
        mixed = jnp.where(lane < 16, low, both - low)
        ident = ident - mixed * pick(ident, k)
        factors = jnp.where((lane == local + k) & (sub > k), mult, factors)
        scale = jnp.where(sub == k, inverse, scale)

    in_block = (lane >= local) & (lane < local + 16)
    lower_of_block = in_block & (lane - local < sub)
    merged = jnp.where(lower_of_block, factors, jnp.where(lane < local, original[half], upper[0]))
    a_ref[half, pl.ds(start, 16), :] = merged
    if half == 0:
        a_ref[1, pl.ds(start, 16), :] = upper[1]
    left_inv = pltpu.roll(jnp.where(lane < 16, ident, 0.0), local, axis=1)
    right_inv = pltpu.roll(
        jnp.where((lane >= 16) & (lane < 32), ident * scale, 0.0), lax.rem(local + NB - 16, NB), axis=1
    )
    zero = jnp.zeros((16, NB), F32)
    xl_ref[half, pl.ds(start, 16), :] = left_inv
    xl_ref[1 - half, pl.ds(start, 16), :] = zero
    xu_ref[half, pl.ds(start, 16), :] = right_inv
    xu_ref[1 - half, pl.ds(start, 16), :] = zero

    t_ref[0, pl.ds(local, 16), :] = jnp.where(
        lane >= local + 16, jordan[0] * scale, jnp.where(in_block, right_inv, 0.0)
    )
    if half == 0:
        t_ref[1, pl.ds(local, 16), :] = jordan[1] * scale
    rows = 2 * NB - half * NB
    below = iota((rows, NB), 0) + half * NB >= start + 16
    wide_lane = iota((rows, NB), 1)
    block_lane = (wide_lane >= local) & (wide_lane < local + 16)
    panel = a_ref[half, half * NB :, :]
    panel_parts = split(panel)
    product = dot3(panel_parts, split(t_ref[0]))
    a_ref[half, half * NB :, :] = jnp.where(
        below, jnp.where(block_lane, product, panel - product), panel
    )
    if half == 0:
        other = a_ref[1]
        product = dot3(panel_parts, split(t_ref[1]))
        a_ref[1] = jnp.where(below, other - product, other)
    t_ref[0, pl.ds(local, 16), :] = zero
    if half == 0:
        t_ref[1, pl.ds(local, 16), :] = zero


def inverses(a_ref, xl_ref, xu_ref):
    packed = jnp.concatenate([a_ref[0], a_ref[1]], 1)
    left = jnp.concatenate([xl_ref[0], xl_ref[1]], 1)
    right = jnp.concatenate([xu_ref[0], xu_ref[1]], 1)
    row = iota((256, 256), 0)
    col = iota((256, 256), 1)
    size = 16
    while size < 256:
        pair = row // (2 * size) == col // (2 * size)
        low_corner = pair & (row % (2 * size) >= size) & (col % (2 * size) < size)
        up_corner = pair & (row % (2 * size) < size) & (col % (2 * size) >= size)
        left_parts = split(left)
        right_parts = split(right)
        first = dot3(left_parts, split(jnp.where(low_corner, packed, 0.0)))
        second = dot3(right_parts, split(jnp.where(up_corner, packed, 0.0)))
        left = left - dot3(split(first), left_parts)
        right = right - dot3(split(second), right_parts)
        size *= 2
    return packed, left, right


def lu_kernel(square_ref, packed_ref, linv_ref, uinv_ref, a_ref, xl_ref, xu_ref, t_ref):
    a_ref[...] = square_ref[...]
    t_ref[...] = jnp.zeros(t_ref.shape, F32)
    for half in range(2):
        def step(index, carry, half=half):
            eliminate(a_ref, xl_ref, xu_ref, t_ref, index, half)
            return carry

        lax.fori_loop(0, 8, step, 0)
    packed, left, right = inverses(a_ref, xl_ref, xu_ref)
    packed_ref[...] = packed
    linv_ref[...] = left
    uinv_ref[...] = right


def lu_call(square):
    result = jax.ShapeDtypeStruct((2 * NB, 2 * NB), F32)
    return pl.pallas_call(
        lu_kernel,
        out_shape=[result] * 3,
        scratch_shapes=[pltpu.VMEM((2, 2 * NB, NB), F32)] * 3 + [pltpu.VMEM((2, NB, NB), F32)],
        compiler_params=pltpu.CompilerParams(vmem_limit_bytes=32 * 2**20),
        name="factor",
    )(square)


def panel_line(number):
    return (number >> 4) * PIECE + NB + (number & 15)


def index_kernel(piv_ref, idx_ref, slot_ref):
    lane = iota((NB, NB), 1).astype(F32)
    sub = iota((NB, NB), 0).astype(F32)

    def rows(x):
        return jnp.broadcast_to(x, (NB, NB))

    def lanes_sum(cond, value=1.0):
        return rows(jnp.sum(jnp.where(cond, value, 0.0), axis=1, keepdims=True))

    def subs_sum(cond, value=1.0):
        return rows(jnp.sum(jnp.where(cond, value, 0.0), axis=0, keepdims=True))

    given = piv_ref[...].astype(F32)
    row = [rows(given[s : s + 1, :]) for s in range(2)]
    col = [x.T for x in row]
    fill_row, fill_col = [], []
    for s in range(2):
        start = float(s * NB)
        listed_row = subs_sum(col[s] == lane + start)
        listed_col = lanes_sum(row[s] == sub + start)
        rank_vacated = lanes_sum((lane <= sub) & (row[s] >= start + NB))
        rank_displaced = subs_sum((sub <= lane) & (listed_col == 0.0))
        pairing = (col[s] >= start + NB) & (listed_row == 0.0) & (rank_vacated == rank_displaced)
        filler = lanes_sum(pairing, lane + start)
        fill_col.append(filler)
        fill_row.append(filler.T)
    again = col[1] == row[0]
    source_col = jnp.where(lanes_sum(again) > 0.0, lanes_sum(again, fill_row[0]), col[1])
    moved = fill_col[1] == row[0]
    second_col = jnp.where(lanes_sum(moved) > 0.0, lanes_sum(moved, fill_row[0]), fill_col[1])

    def whole(x):
        return x.astype(jnp.int32)

    def place(value):
        number = whole(value)
        return (number >> 7) & 3, (number >> 9) * NB + (number & (NB - 1))

    def ranks(keys):
        keys_row = [k.astype(F32) for k in keys]
        keys_col = [k.T for k in keys_row]
        first = subs_sum((keys_col[0] == keys_row[0]) & (sub < lane))
        second = subs_sum((keys_col[1] == keys_row[1]) & (sub < lane)) + subs_sum(
            keys_col[0] == keys_row[1]
        )
        return [whole(first), whole(second)]

    sources = [row[0], source_col.T]
    owners, locals_ = zip(*[place(x) for x in sources])
    rank_arr = ranks(owners)
    slots = [o * SLOTS_A + r for o, r in zip(owners, rank_arr)]
    valid = [(row[0] >= 2.0 * NB) & (subs_sum(again) == 0.0), row[1] >= 2.0 * NB]
    origins = [whole(fill_row[0]), whole(second_col.T)]
    dests, targets = zip(*[place(x) for x in row])
    halves = [x >> 7 for x in origins]
    keys = [jnp.where(v, h * 4 + d, 9) for v, h, d in zip(valid, halves, dests)]
    rank_disp = ranks(keys)
    zero = jnp.zeros((NB, NB), jnp.int32)
    over = zero
    for g in range(2):
        over = over + whole(rows(jnp.sum(jnp.where(rank_arr[g] >= SLOTS_A, 1.0, 0.0), axis=1, keepdims=True)))
        bad = valid[g] & (rank_disp[g] >= SLOTS_D)
        over = over + whole(rows(jnp.sum(jnp.where(bad, 1.0, 0.0), axis=1, keepdims=True)))
    me = lax.axis_index("prow")

    def compact(chosen, values):
        chosen = [jnp.where(c, 1.0, 0.0) for c in chosen]
        chosen_col = [c.T for c in chosen]
        first = subs_sum((chosen_col[0] > 0.0) & (sub < lane))
        total = subs_sum(chosen_col[0] > 0.0)
        second = subs_sum((chosen_col[1] > 0.0) & (sub < lane)) + total
        order = [jnp.where(c > 0.0, r, -1.0).T for c, r in zip(chosen, (first, second))]
        packed = []
        for value in values:
            value_col = [v.astype(F32).T for v in value]
            packed.append(
                [
                    whole(sum(subs_sum(o == lane + g * NB, v) for o, v in zip(order, value_col)))
                    for g in range(2)
                ]
            )
        count = whole(total + subs_sum(chosen_col[1] > 0.0))
        return packed, [count, count]

    (arr_local,), _ = compact([o == me for o in owners], [locals_])
    out_slot = [
        jnp.where(v & (h == me), d * SLOTS_D + r, -1).astype(F32).T
        for v, h, d, r in zip(valid, halves, dests, rank_disp)
    ]
    out_row = [(x & (NB - 1)).astype(F32).T for x in origins]
    out_local = [
        whole(sum(subs_sum(o == lane + g * NB, v) for o, v in zip(out_slot, out_row))) for g in range(2)
    ]
    (in_target, in_row, in_line, in_origin), in_count = compact(
        [v & (d == me) for v, d in zip(valid, dests)],
        [
            targets,
            [h * NB + r for h, r in zip(halves, rank_disp)],
            [panel_line(h * SLOTS_D + r) for h, r in zip(halves, rank_disp)],
            origins,
        ],
    )
    fields = [
        owners, locals_, [over, over], arr_local, out_local,
        in_target, in_row, in_line, in_origin, in_count,
    ]
    for number, field in enumerate(fields):
        for g in range(2):
            idx_ref[number : number + 1, g * NB : (g + 1) * NB] = field[g][0:1, :]
    for number in range(len(fields), 16):
        idx_ref[number : number + 1, :] = jnp.zeros((1, 2 * NB), jnp.int32)
    for g in range(2):
        slot_ref[g * NB : (g + 1) * NB, :] = whole(slots[g].astype(F32).T)


def index_call(pivots):
    return pl.pallas_call(
        index_kernel,
        out_shape=[
            jax.ShapeDtypeStruct((16, 2 * NB), jnp.int32),
            jax.ShapeDtypeStruct((2 * NB, NB), jnp.int32),
        ],
        name="indices",
    )(pivots)


ANY = pl.BlockSpec(memory_space=pl.ANY)


def rows8(start, size):
    return pl.ds(pl.multiple_of(start, 8), size)


def front_kernel(
    idx_ref, slot_ref, x_ref, recv_arr, recv_disp, panel, packed_ref, linv_ref, uinv_ref,
    whole, top, arr_ref, disp_ref, arr_line_ref, disp_line_ref, raw_ref, arr_buf, disp_buf, square,
    a_ref, xl_ref, xu_ref, t_ref,
    load_sem, local_sem, y_send, y_recv, p_send, p_recv, t_send, t_recv, s_send, s_recv,
    scatter_send, scatter_recv, x_send, x_recv, z_send, z_recv, pair_send, pair_recv,
):
    lines = whole.shape[0] // (16 * NB)
    size = whole.shape[0] // LOADS
    load_top = pltpu.make_async_copy(x_ref.at[pl.ds(0, NB * lines)], top, local_sem.at[5])
    load_top.start()
    loads = []
    for number in range(LOADS):
        here = pl.ds(number * size, size)
        loads.append(pltpu.make_async_copy(x_ref.at[here], whole.at[here], load_sem.at[number]))
        loads[-1].start()
    p = lax.axis_index("prow")
    q = lax.axis_index("pcol")
    cx, cz, core = q // 8, (q // 2) % 4, q % 2
    root = q < 2

    def column(ix, iz, icore):
        return (ix % 4 * 4 + iz % 4) * 2 + icore

    up, down, across = ((p + 1) % 4, q), ((p + 3) % 4, q), ((p + 2) % 4, q)
    sibling = (p, column(cx, cz, 1 - core))
    x_peers = [(p, column(cx + i, cz, core)) for i in (1, 2, 3)]
    z_peers = [(p, column(cx, cz + i, core)) for i in (1, 2, 3)]
    near = [up, down, across, sibling] + x_peers + z_peers
    barrier = pltpu.get_barrier_semaphore()
    for other in near:
        pl.semaphore_signal(barrier, inc=1, device_id=other, device_id_type=MESH)

    @pl.when((cx > 0) & (cz > 0))
    def _():
        pl.semaphore_signal(barrier, inc=1, device_id=(p, core), device_id_type=MESH)

    def remote(src, dst, send, recv, device):
        return pltpu.make_async_remote_copy(
            src_ref=src, dst_ref=dst, send_sem=send, recv_sem=recv, device_id=device, device_id_type=MESH
        )

    load_top.wait()

    def displaced(t, carry):
        disp_ref[pl.ds(t * lines, lines), :] = top[pl.ds(idx_ref[OUT_LOCAL, t] * lines, lines), :]
        return carry

    def arriving(j, carry):
        arr_ref[pl.ds(j * lines, lines), :] = whole[pl.ds(idx_ref[ARR_LOCAL, j] * lines, lines), :]
        return carry

    @pl.when(p < 2)
    def _():
        lax.fori_loop(0, 4 * SLOTS_D, displaced, 0, unroll=4)
        disp_line_ref[...] = disp_ref[pl.ds(0, 4 * SLOTS_D, lines), :]

    pl.semaphore_wait(barrier, jnp.where(root, len(near) + 9, len(near)))

    def arr_lines(owner):
        return arr_buf.at[rows8(owner * SLOTS_A, SLOTS_A)]

    def disp_lines(half):
        return disp_buf.at[rows8(half * SLOTS_D, SLOTS_D)]

    def disp_for(owner):
        return disp_line_ref.at[rows8(owner * SLOTS_D, SLOTS_D)]

    peers = [up, down, across]
    own_arr = pltpu.make_async_copy(arr_line_ref, arr_lines(p), local_sem.at[1])
    own_disp = pltpu.make_async_copy(disp_for(p), disp_lines(p % 2), local_sem.at[2])
    arr_panel = [remote(arr_line_ref, arr_lines(p), p_send.at[i], p_recv.at[i], peers[i]) for i in range(3)]
    disp_panel = [
        remote(disp_for(peers[i][0]), disp_lines(p % 2), p_send.at[3 + i], p_recv.at[3 + p % 2], peers[i])
        for i in range(3)
    ]

    @pl.when(root & (p < 2))
    def _():
        for copy in disp_panel:
            copy.start()
        own_disp.start()

    arr_size, disp_size = arr_ref.shape[0], disp_ref.shape[0] // 4
    half_size = arr_size // 2
    low, high = pl.ds(0, half_size), pl.ds(half_size, half_size)

    def arr_rows(owner, part):
        return recv_arr.at[rows8(owner * arr_size + part.start, part.size)]

    def moved_to(owner):
        return disp_ref.at[rows8(owner * disp_size, disp_size)]

    def moved(half):
        return recv_disp.at[rows8(half * (recv_disp.shape[0] // 2), disp_size)]

    own_rows = pltpu.make_async_copy(arr_ref, recv_arr.at[rows8(p * arr_size, arr_size)], local_sem.at[3])
    own_moved = pltpu.make_async_copy(moved_to(p), moved(p % 2), local_sem.at[4])
    bulk = [
        remote(arr_ref.at[low], arr_rows(p, low), y_send.at[0], y_recv.at[0], up),
        remote(arr_ref.at[high], arr_rows(p, high), y_send.at[1], y_recv.at[1], down),
        remote(arr_ref.at[high], arr_rows(p, high), y_send.at[2], y_recv.at[2], up),
        remote(arr_ref.at[low], arr_rows(p, low), y_send.at[3], y_recv.at[3], down),
    ]
    half = p % 2
    to_up = remote(moved_to(up[0]), moved(half), y_send.at[4], y_recv.at[4 + half], up)
    to_down = remote(moved_to(down[0]), moved(half), y_send.at[5], y_recv.at[4 + half], down)
    to_across = remote(moved_to(across[0]), moved(half), y_send.at[6], y_recv.at[4 + half], across)

    @pl.when(p < 2)
    def _():
        to_across.start()
        own_moved.start()

    forward = [
        remote(arr_rows(down[0], low), arr_rows(down[0], low), y_send.at[7], y_recv.at[7], up),
        remote(arr_rows(up[0], high), arr_rows(up[0], high), y_send.at[8], y_recv.at[8], down),
    ]
    for load in loads:
        load.wait()
    lax.fori_loop(0, SLOTS_A, arriving, 0, unroll=4)
    arr_line_ref[...] = arr_ref[pl.ds(0, SLOTS_A, lines), :]

    @pl.when(root)
    def _():
        for copy in arr_panel:
            copy.start()
        own_arr.start()

    for copy in bulk[:2]:
        copy.start()
    own_rows.start()

    upper, lower = square.at[core, pl.ds(0, NB)], square.at[core, pl.ds(NB, NB)]
    upper_x = [remote(upper, upper, t_send.at[0, i], t_recv.at[0], x_peers[i]) for i in range(3)]
    lower_z = [remote(lower, lower, t_send.at[1, i], t_recv.at[1], z_peers[i]) for i in range(3)]
    upper_z = [remote(upper, upper, t_send.at[2, i], t_recv.at[0], z_peers[i]) for i in range(3)]
    lower_x = [remote(lower, lower, t_send.at[3, i], t_recv.at[1], x_peers[i]) for i in range(3)]
    own_square = remote(square.at[core], square.at[core], s_send.at[0], s_recv.at[0], sibling)

    start, end = pl.ds(0, PIECE // 2), pl.ds(PIECE // 2, PIECE // 2)
    scatter = [
        remote(
            raw_ref.at[i], panel.at[core, i // 4, i % 4], scatter_send.at[i - 1], scatter_recv.at[0],
            (p, column(i // 4, i % 4, core)),
        )
        for i in range(1, 16)
    ]
    own_piece = pltpu.make_async_copy(raw_ref.at[0], panel.at[core, 0, 0], local_sem.at[0])
    along = []
    for i in range(3):
        mine_low, mine_high = panel.at[core, cx, cz, start], panel.at[core, cx, cz, end]
        along.append(remote(mine_low, mine_low, x_send.at[0, i], x_recv.at[0, i], x_peers[i]))
        along.append(remote(mine_high, mine_high, z_send.at[0, i], z_recv.at[0, i], z_peers[i]))
    spread = []
    for i in range(3):
        mine_low, mine_high = panel.at[core, :, cz, start], panel.at[core, cx, :, end]
        spread.append(remote(mine_low, mine_low, z_send.at[1, i], z_recv.at[1, i], z_peers[i]))
        spread.append(remote(mine_high, mine_high, x_send.at[1, i], x_recv.at[1, i], x_peers[i]))
    pair = remote(panel.at[core], panel.at[core], pair_send.at[0], pair_recv.at[0], sibling)

    @pl.when(root)
    def _():
        for i in range(16):
            raw_ref[i, :NB] = whole[pl.ds(i * NB * lines, NB, lines), :]
        own_arr.wait()
        for copy in arr_panel:
            copy.wait_recv()
        onehot = jnp.where(iota((2 * NB, 4 * SLOTS_A), 1) == slot_ref[:, :1], 1.0, 0.0).astype(BF16)
        square[core] = onehot_rows(onehot, arr_buf[...])
        for copy in upper_x + lower_z:
            copy.start()

    @pl.when(jnp.logical_not(root))
    def _():
        upper_x[0].wait_recv()

    @pl.when(cz == 0)
    def _():
        for copy in upper_z:
            copy.start()

    @pl.when(jnp.logical_not(root))
    def _():
        lower_z[0].wait_recv()

    @pl.when(cx == 0)
    def _():
        for copy in lower_x:
            copy.start()

    own_square.start()

    @pl.when(root)
    def _():
        for source in range(2):
            @pl.when(p == source)
            def _():
                own_disp.wait()

            @pl.when(p != source)
            def _(source=source):
                remote(disp_for(0), disp_lines(source), p_send.at[3], p_recv.at[3 + source], up).wait_recv()
        for i in range(16):
            raw_ref[i, NB:] = disp_buf[i * 16 : i * 16 + 16, :] if i * 16 < 2 * SLOTS_D else jnp.zeros((16, NB), F32)
        for copy in scatter:
            copy.start()
        own_piece.start()

    for copy in bulk[2:]:
        copy.start()

    @pl.when(p < 2)
    def _():
        to_up.start()
        to_down.start()

    own_square.wait_recv()
    a_ref[...] = square[...]
    t_ref[...] = jnp.zeros(t_ref.shape, F32)

    def pass_rows():
        bulk[0].wait_recv()
        forward[0].start()
        bulk[1].wait_recv()
        forward[1].start()

    def pass_piece():
        @pl.when(root)
        def _():
            own_piece.wait()

        @pl.when(jnp.logical_not(root))
        def _():
            scatter[0].wait_recv()

        for copy in along:
            copy.start()

    def pass_pieces():
        for copy in along:
            copy.wait_recv()
        for copy in spread:
            copy.start()

    def pass_panel():
        for copy in spread:
            copy.wait_recv()
        pair.start()

    events = [{2: pass_piece, 3: pass_rows, 6: pass_pieces}, {6: pass_panel}]
    for half_number in range(2):
        def factor_step(index, carry, half_number=half_number):
            for when, event in events[half_number].items():
                pl.when(index == when)(event)
            eliminate(a_ref, xl_ref, xu_ref, t_ref, index, half_number)
            return carry

        lax.fori_loop(0, 8, factor_step, 0)
    packed, left, right = inverses(a_ref, xl_ref, xu_ref)
    packed_ref[...] = packed
    linv_ref[...] = left
    uinv_ref[...] = right

    bulk[2].wait_recv()
    bulk[3].wait_recv()
    for copy in forward:
        copy.wait_recv()
    own_rows.wait()
    for source in range(2):
        @pl.when(p == source)
        def _():
            own_moved.wait()

        @pl.when(p != source)
        def _(source=source):
            remote(moved_to(0), moved(source), y_send.at[4], y_recv.at[4 + source], up).wait_recv()
    pair.wait_recv()
    for copy in bulk + forward + along + spread + [pair]:
        copy.wait_send()

    @pl.when(p < 2)
    def _():
        to_up.wait_send()
        to_down.wait_send()
        to_across.wait_send()

    @pl.when(cz == 0)
    def _():
        for copy in upper_z:
            copy.wait_send()

    @pl.when(cx == 0)
    def _():
        for copy in lower_x:
            copy.wait_send()

    own_square.wait_send()

    @pl.when(root)
    def _():
        for copy in arr_panel + upper_x + lower_z + scatter:
            copy.wait_send()

        @pl.when(p < 2)
        def _():
            for copy in disp_panel:
                copy.wait_send()


def front_call(idx, slot, x, lines):
    dma = pltpu.SemaphoreType.DMA
    vmem = pl.BlockSpec(memory_space=pltpu.VMEM)
    result = jax.ShapeDtypeStruct((2 * NB, 2 * NB), F32)
    sizes = [(4 * SLOTS_A * lines,), (2 * NB * lines,), (2, 4, 4, PIECE)]
    held = [
        x.shape[:1], (NB * lines,), (SLOTS_A * lines,), (4 * SLOTS_D * lines,), (SLOTS_A,), (4 * SLOTS_D,), (16, PIECE),
        (4 * SLOTS_A,), (2 * SLOTS_D,), (2, 2 * NB), (2, 2 * NB), (2, 2 * NB), (2, 2 * NB), (2, NB),
    ]
    semaphores = [
        (LOADS,), (6,), (9,), (9,), (6,), (5,), (4, 3), (2,), (1,), (1,),
        (15,), (1,), (2, 3), (2, 3), (2, 3), (2, 3), (1,), (1,),
    ]
    return pl.pallas_call(
        front_kernel,
        in_specs=[pl.BlockSpec(memory_space=pltpu.SMEM), vmem, ANY],
        out_specs=[ANY] * 3 + [vmem] * 3,
        out_shape=[jax.ShapeDtypeStruct(size + (NB,), F32) for size in sizes] + [result] * 3,
        scratch_shapes=[pltpu.VMEM(size + (NB,), F32) for size in held] + [dma(shape) for shape in semaphores],
        compiler_params=pltpu.CompilerParams(
            collective_id=0, has_side_effects=True, vmem_limit_bytes=48 * 2**20
        ),
        name="front",
    )(idx, slot, x)


STEP_ROWS = 256


def update_kernel(
    idx_ref, x_ref, panel_ref, disp_ref, arr_ref, slot_ref, packed_ref, linv_ref, uinv_ref, o_ref,
    whole, pan, stacked, u_ref, x_sem, pan_sem,
):
    p = lax.axis_index("prow")
    q = lax.axis_index("pcol")
    step = pl.program_id(0)
    lines = whole.shape[0] // (16 * NB)

    @pl.when(step == 0)
    def _():
        load = pltpu.make_async_copy(x_ref, whole, x_sem)
        load.start()
        load_panel = pltpu.make_async_copy(panel_ref, pan, pan_sem)
        load_panel.start()
        high, low = split(linv_ref[...])
        slot = slot_ref[:, :1]
        onehot = jnp.where(iota((2 * NB, 4 * SLOTS_A), 1) == slot, 1.0, 0.0).astype(BF16)
        left = (dot(high, onehot).astype(BF16), dot(low, onehot).astype(BF16))
        for c in range(lines):
            rows = arr_ref[pl.ds(c, 4 * SLOTS_A, lines), :]
            value = dot3(left, split(rows))
            here = slice(c * NB, (c + 1) * NB)
            u_ref[:, here] = value
            upper, rest = split(value)
            stacked[0 : 2 * NB, here] = upper
            stacked[2 * NB : 4 * NB, here] = rest
            stacked[4 * NB : 6 * NB, here] = upper
        load_panel.wait()
        load.wait()

        def patch(t, carry):
            target = idx_ref[IN_TARGET, t]
            line = idx_ref[IN_LINE, t]
            panel_row = (target >> 7) * PIECE + (target & (NB - 1))
            for half in range(2):
                pan[half, pl.ds(panel_row, 1), :] = pan[half, pl.ds(line, 1), :]
            source = idx_ref[IN_ROW, t] * lines
            whole[pl.ds(target * lines, lines), :] = disp_ref[pl.ds(source, lines), :]
            return carry

        lax.fori_loop(0, idx_ref[IN_COUNT, 0], patch, 0)

    rows = []
    for number in range(STEP_ROWS // NB):
        here = pl.ds(pl.multiple_of((step * (STEP_ROWS // NB) + number) * PIECE, 8), NB)
        rows.append(jnp.concatenate([pan[0, here, :], pan[1, here, :]], 1))
    rows = jnp.concatenate(rows, 0)
    mult = dot3(split(rows), split(uinv_ref[...]))
    high, low = split(mult)
    left = jnp.concatenate([high, high, low], 1)
    base = step * (STEP_ROWS * lines)
    for c in range(0, lines, 2):
        product = dot(left, stacked[:, c * NB : (c + 2) * NB])
        for k in range(2):
            current = whole[pl.ds(base + c + k, STEP_ROWS, lines), :]
            o_ref[pl.ds(c + k, STEP_ROWS, lines), :] = current - product[:, k * NB : (k + 1) * NB]

    for half in range(2):
        @pl.when(q == half)
        def _(half=half):
            o_ref[pl.ds(0, STEP_ROWS, lines), :] = mult[:, half * NB : (half + 1) * NB]

    for half in range(2):
        @pl.when((p == half) & (step == 0))
        def _(half=half):
            top = slice(half * NB, (half + 1) * NB)
            for c in range(lines):
                value = u_ref[top, c * NB : (c + 1) * NB]
                if c == 0:
                    value = jnp.where(q == 0, packed_ref[top, :NB], jnp.where(q == 1, packed_ref[top, NB:], value))
                o_ref[pl.ds(c, NB, lines), :] = value


def update_call(idx, x, panel, disp, arr, slot, packed, linv, uinv, lines):
    vmem = pl.BlockSpec(memory_space=pltpu.VMEM)
    return pl.pallas_call(
        update_kernel,
        grid=(16 * NB // STEP_ROWS,),
        in_specs=[pl.BlockSpec(memory_space=pltpu.SMEM), ANY, ANY] + [vmem] * 6,
        out_specs=pl.BlockSpec((STEP_ROWS * lines, NB), lambda i: (i, 0)),
        out_shape=jax.ShapeDtypeStruct((16 * NB * lines, NB), F32),
        scratch_shapes=[
            pltpu.VMEM((16 * NB * lines, NB), F32),
            pltpu.VMEM((2, 16 * PIECE, NB), F32),
            pltpu.VMEM((6 * NB, NB * lines), BF16),
            pltpu.VMEM((2 * NB, NB * lines), F32),
            pltpu.SemaphoreType.DMA,
            pltpu.SemaphoreType.DMA,
        ],
        compiler_params=pltpu.CompilerParams(vmem_limit_bytes=48 * 2**20),
        name="update",
    )(idx, x, panel, disp, arr, slot, packed, linv, uinv)


def shards(matrix, pivots):
    lines = matrix.shape[3]
    rows = matrix.shape[0] * NB
    p = lax.axis_index("prow")
    q = lax.axis_index("pcol")
    x = matrix.reshape(rows * lines, NB)
    idx, slot = index_call(pivots)

    def total(x, axis, count):
        bit = 1
        while bit < count:
            x = x + lax.ppermute(x, axis, [(i, i ^ bit) for i in range(count)])
            bit *= 2
        return x

    def fits(x, idx, slot):
        recv_arr, recv_disp, panel, packed, linv, uinv = front_call(idx, slot, x, lines)
        return recv_arr, recv_disp, panel, packed, linv, uinv, idx, slot

    def general(x, idx, slot):
        x = x.reshape(rows, lines, NB)
        chosen = jnp.where((idx[OWNER] == p)[:, None, None], jnp.take(x, idx[LOCAL], axis=0), 0.0)
        top = jnp.concatenate([jnp.where(p == s, x[:NB], 0.0) for s in range(2)])
        chosen, top = total(chosen, "prow", 4), total(top, "prow", 4)
        own = jnp.concatenate([x[:, 0].reshape(16, NB, NB), top[:, 0].reshape(16, 16, NB)], 1)
        own = jnp.concatenate([own.reshape(-1, NB), chosen[:, 0]])
        both = total(jnp.stack([jnp.where(q == s, own, 0.0) for s in range(2)]), "pcol", 32)
        panel = both[:, : 16 * PIECE].reshape(2, 4, 4, PIECE, NB)
        order = jnp.arange(2 * NB, dtype=jnp.int32)
        idx = idx.at[IN_ROW].set(idx[IN_ORIGIN]).at[IN_LINE].set(panel_line(idx[IN_ORIGIN]))
        slot = jnp.broadcast_to(order[:, None], slot.shape)
        packed, linv, uinv = lu_call(both[:, 16 * PIECE :])
        chosen = jnp.pad(chosen, ((0, 4 * SLOTS_A - 2 * NB), (0, 0), (0, 0)))
        return chosen.reshape(-1, NB), top.reshape(-1, NB), panel, packed, linv, uinv, idx, slot

    arr, disp, panel, packed, linv, uinv, idx, slot = lax.cond(idx[OVER, 0] == 0, fits, general, x, idx, slot)
    panel = panel.reshape(2, -1, NB)
    out = update_call(idx, x, panel, disp, arr, slot, packed, linv, uinv, lines)
    return out.reshape(matrix.shape)


def solution(mesh):
    placed = (P(None, "prow", None, None, "pcol", None), P())
    return jax.shard_map(
        shards,
        mesh=mesh,
        in_specs=placed,
        out_specs=P(None, "prow", None, None, "pcol", None),
        check_vma=False,
    )
```

```python
import jax
import jax.numpy as jnp
from jax import lax
from jax.experimental import pallas as pl
from jax.experimental.pallas import tpu as pltpu
from jax.sharding import PartitionSpec as P

NB = 128
F32 = jnp.float32
BF16 = jnp.bfloat16
MESH = pl.DeviceIdType.MESH
SLOTS_A = 88
SLOTS_D = 56
LOADS = 16
PIECE = NB + 16
(
    OWNER, LOCAL, OVER, ARR_LOCAL, OUT_LOCAL, IN_TARGET, IN_ROW, IN_LINE, IN_ORIGIN, IN_COUNT,
) = range(10)


def split(x):
    high = x.astype(BF16)
    return high, (x - high.astype(F32)).astype(BF16)


def dot(a, b):
    return jnp.dot(a, b, preferred_element_type=F32)


def dot3(a, b):
    ah, al = a
    bh, bl = b
    return dot(ah, bh) + (dot(ah, bl) + dot(al, bh))


def onehot_rows(onehot, x):
    high = x.astype(BF16)
    rest = x - high.astype(F32)
    mid = rest.astype(BF16)
    low = (rest - mid.astype(F32)).astype(BF16)
    return (dot(onehot, high) + dot(onehot, mid)) + dot(onehot, low)


def iota(shape, dim):
    return lax.broadcasted_iota(jnp.int32, shape, dim)


def eliminate(a_ref, xl_ref, xu_ref, t_ref, index, half):
    local = pl.multiple_of(index * 16, 16)
    start = pl.multiple_of(half * NB + local, 16)
    sub = iota((16, NB), 0)
    lane = iota((16, NB), 1)
    original = [a_ref[g, pl.ds(start, 16), :] for g in range(2)]
    rolled = pltpu.roll(original[half], lax.rem(NB - local, NB), axis=1)
    cols = [jnp.broadcast_to(rolled[:, j : j + 1], (16, NB)) for j in range(16)]
    upper = list(original[half:])
    jordan = list(original[half:])
    ident = jnp.where((lane == sub) | (lane == sub + 16), 1.0, 0.0).astype(F32)
    factors = jnp.zeros((16, NB), F32)
    scale = jnp.zeros((16, NB), F32)

    def pick(x, k):
        return jnp.broadcast_to(x[k : k + 1, :], (16, NB))

    for k in range(16):
        inverse = 1.0 / pick(cols[k], k)
        mult = cols[k] * inverse
        low = jnp.where(sub > k, mult, 0.0)
        both = jnp.where(sub != k, mult, 0.0)
        for j in range(k + 1, 16):
            cols[j] = cols[j] - both * pick(cols[j], k)
        upper = [x - low * pick(x, k) for x in upper]
        jordan = [x - both * pick(x, k) for x in jordan]
        mixed = jnp.where(lane < 16, low, both - low)
        ident = ident - mixed * pick(ident, k)
        factors = jnp.where((lane == local + k) & (sub > k), mult, factors)
        scale = jnp.where(sub == k, inverse, scale)

    in_block = (lane >= local) & (lane < local + 16)
    lower_of_block = in_block & (lane - local < sub)
    merged = jnp.where(lower_of_block, factors, jnp.where(lane < local, original[half], upper[0]))
    a_ref[half, pl.ds(start, 16), :] = merged
    if half == 0:
        a_ref[1, pl.ds(start, 16), :] = upper[1]
    left_inv = pltpu.roll(jnp.where(lane < 16, ident, 0.0), local, axis=1)
    right_inv = pltpu.roll(
        jnp.where((lane >= 16) & (lane < 32), ident * scale, 0.0), lax.rem(local + NB - 16, NB), axis=1
    )
    zero = jnp.zeros((16, NB), F32)
    xl_ref[half, pl.ds(start, 16), :] = left_inv
    xl_ref[1 - half, pl.ds(start, 16), :] = zero
    xu_ref[half, pl.ds(start, 16), :] = right_inv
    xu_ref[1 - half, pl.ds(start, 16), :] = zero

    t_ref[0, pl.ds(local, 16), :] = jnp.where(
        lane >= local + 16, jordan[0] * scale, jnp.where(in_block, right_inv, 0.0)
    )
    if half == 0:
        t_ref[1, pl.ds(local, 16), :] = jordan[1] * scale
    rows = 2 * NB - half * NB
    below = iota((rows, NB), 0) + half * NB >= start + 16
    wide_lane = iota((rows, NB), 1)
    block_lane = (wide_lane >= local) & (wide_lane < local + 16)
    panel = a_ref[half, half * NB :, :]
    panel_parts = split(panel)
    product = dot3(panel_parts, split(t_ref[0]))
    a_ref[half, half * NB :, :] = jnp.where(
        below, jnp.where(block_lane, product, panel - product), panel
    )
    if half == 0:
        other = a_ref[1]
        product = dot3(panel_parts, split(t_ref[1]))
        a_ref[1] = jnp.where(below, other - product, other)
    t_ref[0, pl.ds(local, 16), :] = zero
    if half == 0:
        t_ref[1, pl.ds(local, 16), :] = zero


def inverses(a_ref, xl_ref, xu_ref):
    packed = jnp.concatenate([a_ref[0], a_ref[1]], 1)
    left = jnp.concatenate([xl_ref[0], xl_ref[1]], 1)
    right = jnp.concatenate([xu_ref[0], xu_ref[1]], 1)
    row = iota((256, 256), 0)
    col = iota((256, 256), 1)
    size = 16
    while size < 256:
        pair = row // (2 * size) == col // (2 * size)
        low_corner = pair & (row % (2 * size) >= size) & (col % (2 * size) < size)
        up_corner = pair & (row % (2 * size) < size) & (col % (2 * size) >= size)
        left_parts = split(left)
        right_parts = split(right)
        first = dot3(left_parts, split(jnp.where(low_corner, packed, 0.0)))
        second = dot3(right_parts, split(jnp.where(up_corner, packed, 0.0)))
        left = left - dot3(split(first), left_parts)
        right = right - dot3(split(second), right_parts)
        size *= 2
    return packed, left, right


def lu_kernel(square_ref, packed_ref, linv_ref, uinv_ref, a_ref, xl_ref, xu_ref, t_ref):
    a_ref[...] = square_ref[...]
    t_ref[...] = jnp.zeros(t_ref.shape, F32)
    for half in range(2):
        def step(index, carry, half=half):
            eliminate(a_ref, xl_ref, xu_ref, t_ref, index, half)
            return carry

        lax.fori_loop(0, 8, step, 0)
    packed, left, right = inverses(a_ref, xl_ref, xu_ref)
    packed_ref[...] = packed
    linv_ref[...] = left
    uinv_ref[...] = right


def lu_call(square):
    result = jax.ShapeDtypeStruct((2 * NB, 2 * NB), F32)
    return pl.pallas_call(
        lu_kernel,
        out_shape=[result] * 3,
        scratch_shapes=[pltpu.VMEM((2, 2 * NB, NB), F32)] * 3 + [pltpu.VMEM((2, NB, NB), F32)],
        compiler_params=pltpu.CompilerParams(vmem_limit_bytes=32 * 2**20),
        name="factor",
    )(square)


def panel_line(number):
    return (number >> 4) * PIECE + NB + (number & 15)


def index_kernel(piv_ref, idx_ref, slot_ref):
    lane = iota((NB, NB), 1).astype(F32)
    sub = iota((NB, NB), 0).astype(F32)

    def rows(x):
        return jnp.broadcast_to(x, (NB, NB))

    def lanes_sum(cond, value=1.0):
        return rows(jnp.sum(jnp.where(cond, value, 0.0), axis=1, keepdims=True))

    def subs_sum(cond, value=1.0):
        return rows(jnp.sum(jnp.where(cond, value, 0.0), axis=0, keepdims=True))

    given = piv_ref[...].astype(F32)
    row = [rows(given[s : s + 1, :]) for s in range(2)]
    col = [x.T for x in row]
    fill_row, fill_col = [], []
    for s in range(2):
        start = float(s * NB)
        listed_row = subs_sum(col[s] == lane + start)
        listed_col = lanes_sum(row[s] == sub + start)
        rank_vacated = lanes_sum((lane <= sub) & (row[s] >= start + NB))
        rank_displaced = subs_sum((sub <= lane) & (listed_col == 0.0))
        pairing = (col[s] >= start + NB) & (listed_row == 0.0) & (rank_vacated == rank_displaced)
        filler = lanes_sum(pairing, lane + start)
        fill_col.append(filler)
        fill_row.append(filler.T)
    again = col[1] == row[0]
    source_col = jnp.where(lanes_sum(again) > 0.0, lanes_sum(again, fill_row[0]), col[1])
    moved = fill_col[1] == row[0]
    second_col = jnp.where(lanes_sum(moved) > 0.0, lanes_sum(moved, fill_row[0]), fill_col[1])

    def whole(x):
        return x.astype(jnp.int32)

    def place(value):
        number = whole(value)
        return (number >> 7) & 3, (number >> 9) * NB + (number & (NB - 1))

    def ranks(keys):
        keys_row = [k.astype(F32) for k in keys]
        keys_col = [k.T for k in keys_row]
        first = subs_sum((keys_col[0] == keys_row[0]) & (sub < lane))
        second = subs_sum((keys_col[1] == keys_row[1]) & (sub < lane)) + subs_sum(
            keys_col[0] == keys_row[1]
        )
        return [whole(first), whole(second)]

    sources = [row[0], source_col.T]
    owners, locals_ = zip(*[place(x) for x in sources])
    rank_arr = ranks(owners)
    slots = [o * SLOTS_A + r for o, r in zip(owners, rank_arr)]
    valid = [(row[0] >= 2.0 * NB) & (subs_sum(again) == 0.0), row[1] >= 2.0 * NB]
    origins = [whole(fill_row[0]), whole(second_col.T)]
    dests, targets = zip(*[place(x) for x in row])
    halves = [x >> 7 for x in origins]
    keys = [jnp.where(v, h * 4 + d, 9) for v, h, d in zip(valid, halves, dests)]
    rank_disp = ranks(keys)
    zero = jnp.zeros((NB, NB), jnp.int32)
    over = zero
    for g in range(2):
        over = over + whole(rows(jnp.sum(jnp.where(rank_arr[g] >= SLOTS_A, 1.0, 0.0), axis=1, keepdims=True)))
        bad = valid[g] & (rank_disp[g] >= SLOTS_D)
        over = over + whole(rows(jnp.sum(jnp.where(bad, 1.0, 0.0), axis=1, keepdims=True)))
    me = lax.axis_index("prow")

    def compact(chosen, values, keys):
        chosen = [jnp.where(c, 1.0, 0.0) for c in chosen]
        chosen_col = [c.T for c in chosen]
        keys_col = [k.T for k in keys]
        before = [
            sum(subs_sum((c > 0.0) & (k < key)) for c, k in zip(chosen_col, keys_col)) for key in keys
        ]
        total = sum(subs_sum(c > 0.0) for c in chosen_col)
        order = [jnp.where(c > 0.0, r, -1.0).T for c, r in zip(chosen, before)]
        packed = []
        for value in values:
            value_col = [v.astype(F32).T for v in value]
            packed.append(
                [
                    whole(sum(subs_sum(o == lane + g * NB, v) for o, v in zip(order, value_col)))
                    for g in range(2)
                ]
            )
        count = whole(total)
        return packed, [count, count]

    (arr_local,), _ = compact([o == me for o in owners], [locals_], [lane, lane + NB])
    out_slot = [
        jnp.where(v & (h == me), d * SLOTS_D + r, -1).astype(F32).T
        for v, h, d, r in zip(valid, halves, dests, rank_disp)
    ]
    out_row = [(x & (NB - 1)).astype(F32).T for x in origins]
    out_local = [
        whole(sum(subs_sum(o == lane + g * NB, v) for o, v in zip(out_slot, out_row))) for g in range(2)
    ]
    (in_target, in_row, in_line, in_origin), in_count = compact(
        [v & (d == me) for v, d in zip(valid, dests)],
        [
            targets,
            [h * NB + r for h, r in zip(halves, rank_disp)],
            [panel_line(h * SLOTS_D + r) for h, r in zip(halves, rank_disp)],
            origins,
        ],
        [t.astype(F32) for t in targets],
    )
    fields = [
        owners, locals_, [over, over], arr_local, out_local,
        in_target, in_row, in_line, in_origin, in_count,
    ]
    for number, field in enumerate(fields):
        for g in range(2):
            idx_ref[number : number + 1, g * NB : (g + 1) * NB] = field[g][0:1, :]
    for number in range(len(fields), 16):
        idx_ref[number : number + 1, :] = jnp.zeros((1, 2 * NB), jnp.int32)
    for g in range(2):
        slot_ref[g * NB : (g + 1) * NB, :] = whole(slots[g].astype(F32).T)


def index_call(pivots):
    return pl.pallas_call(
        index_kernel,
        out_shape=[
            jax.ShapeDtypeStruct((16, 2 * NB), jnp.int32),
            jax.ShapeDtypeStruct((2 * NB, NB), jnp.int32),
        ],
        name="indices",
    )(pivots)


ANY = pl.BlockSpec(memory_space=pl.ANY)


def rows8(start, size):
    return pl.ds(pl.multiple_of(start, 8), size)


def front_kernel(
    idx_ref, slot_ref, x_ref, recv_arr, recv_disp, panel, packed_ref, linv_ref, uinv_ref,
    whole, top, arr_ref, disp_ref, arr_line_ref, disp_line_ref, raw_ref, arr_buf, disp_buf, square,
    a_ref, xl_ref, xu_ref, t_ref,
    load_sem, local_sem, y_send, y_recv, p_send, p_recv, t_send, t_recv, s_send, s_recv,
    scatter_send, scatter_recv, x_send, x_recv, z_send, z_recv, pair_send, pair_recv,
):
    lines = whole.shape[0] // (16 * NB)
    size = whole.shape[0] // LOADS
    load_top = pltpu.make_async_copy(x_ref.at[pl.ds(0, NB * lines)], top, local_sem.at[5])
    load_top.start()
    loads = []
    for number in range(LOADS):
        here = pl.ds(number * size, size)
        loads.append(pltpu.make_async_copy(x_ref.at[here], whole.at[here], load_sem.at[number]))
        loads[-1].start()
    p = lax.axis_index("prow")
    q = lax.axis_index("pcol")
    cx, cz, core = q // 8, (q // 2) % 4, q % 2
    root = q < 2

    def column(ix, iz, icore):
        return (ix % 4 * 4 + iz % 4) * 2 + icore

    up, down, across = ((p + 1) % 4, q), ((p + 3) % 4, q), ((p + 2) % 4, q)
    sibling = (p, column(cx, cz, 1 - core))
    x_peers = [(p, column(cx + i, cz, core)) for i in (1, 2, 3)]
    z_peers = [(p, column(cx, cz + i, core)) for i in (1, 2, 3)]
    near = [up, down, across, sibling] + x_peers + z_peers
    barrier = pltpu.get_barrier_semaphore()
    for other in near:
        pl.semaphore_signal(barrier, inc=1, device_id=other, device_id_type=MESH)

    @pl.when((cx > 0) & (cz > 0))
    def _():
        pl.semaphore_signal(barrier, inc=1, device_id=(p, core), device_id_type=MESH)

    def remote(src, dst, send, recv, device):
        return pltpu.make_async_remote_copy(
            src_ref=src, dst_ref=dst, send_sem=send, recv_sem=recv, device_id=device, device_id_type=MESH
        )

    load_top.wait()

    def displaced(t, carry):
        disp_ref[pl.ds(t * lines, lines), :] = top[pl.ds(idx_ref[OUT_LOCAL, t] * lines, lines), :]
        return carry

    def arriving(j, carry):
        arr_ref[pl.ds(j * lines, lines), :] = whole[pl.ds(idx_ref[ARR_LOCAL, j] * lines, lines), :]
        return carry

    @pl.when(p < 2)
    def _():
        lax.fori_loop(0, 4 * SLOTS_D, displaced, 0, unroll=4)
        disp_line_ref[...] = disp_ref[pl.ds(0, 4 * SLOTS_D, lines), :]

    pl.semaphore_wait(barrier, jnp.where(root, len(near) + 9, len(near)))

    def arr_lines(owner):
        return arr_buf.at[rows8(owner * SLOTS_A, SLOTS_A)]

    def disp_lines(half):
        return disp_buf.at[rows8(half * SLOTS_D, SLOTS_D)]

    def disp_for(owner):
        return disp_line_ref.at[rows8(owner * SLOTS_D, SLOTS_D)]

    peers = [up, down, across]
    own_arr = pltpu.make_async_copy(arr_line_ref, arr_lines(p), local_sem.at[1])
    own_disp = pltpu.make_async_copy(disp_for(p), disp_lines(p % 2), local_sem.at[2])
    arr_panel = [remote(arr_line_ref, arr_lines(p), p_send.at[i], p_recv.at[i], peers[i]) for i in range(3)]
    disp_panel = [
        remote(disp_for(peers[i][0]), disp_lines(p % 2), p_send.at[3 + i], p_recv.at[3 + p % 2], peers[i])
        for i in range(3)
    ]

    @pl.when(root & (p < 2))
    def _():
        for copy in disp_panel:
            copy.start()
        own_disp.start()

    arr_size, disp_size = arr_ref.shape[0], disp_ref.shape[0] // 4
    half_size = arr_size // 2
    low, high = pl.ds(0, half_size), pl.ds(half_size, half_size)

    def arr_rows(owner, part):
        return recv_arr.at[rows8(owner * arr_size + part.start, part.size)]

    def moved_to(owner):
        return disp_ref.at[rows8(owner * disp_size, disp_size)]

    def moved(half):
        return recv_disp.at[rows8(half * (recv_disp.shape[0] // 2), disp_size)]

    own_rows = pltpu.make_async_copy(arr_ref, recv_arr.at[rows8(p * arr_size, arr_size)], local_sem.at[3])
    own_moved = pltpu.make_async_copy(moved_to(p), moved(p % 2), local_sem.at[4])
    bulk = [
        remote(arr_ref.at[low], arr_rows(p, low), y_send.at[0], y_recv.at[0], up),
        remote(arr_ref.at[high], arr_rows(p, high), y_send.at[1], y_recv.at[1], down),
        remote(arr_ref.at[high], arr_rows(p, high), y_send.at[2], y_recv.at[2], up),
        remote(arr_ref.at[low], arr_rows(p, low), y_send.at[3], y_recv.at[3], down),
    ]
    half = p % 2
    to_up = remote(moved_to(up[0]), moved(half), y_send.at[4], y_recv.at[4 + half], up)
    to_down = remote(moved_to(down[0]), moved(half), y_send.at[5], y_recv.at[4 + half], down)
    to_across = remote(moved_to(across[0]), moved(half), y_send.at[6], y_recv.at[4 + half], across)

    @pl.when(p < 2)
    def _():
        to_across.start()
        own_moved.start()

    forward = [
        remote(arr_rows(down[0], low), arr_rows(down[0], low), y_send.at[7], y_recv.at[7], up),
        remote(arr_rows(up[0], high), arr_rows(up[0], high), y_send.at[8], y_recv.at[8], down),
    ]
    for load in loads:
        load.wait()
    lax.fori_loop(0, SLOTS_A, arriving, 0, unroll=4)
    arr_line_ref[...] = arr_ref[pl.ds(0, SLOTS_A, lines), :]

    @pl.when(root)
    def _():
        for copy in arr_panel:
            copy.start()
        own_arr.start()

    for copy in bulk:
        copy.start()
    own_rows.start()

    @pl.when(p < 2)
    def _():
        to_up.start()
        to_down.start()

    upper, lower = square.at[core, pl.ds(0, NB)], square.at[core, pl.ds(NB, NB)]
    upper_x = [remote(upper, upper, t_send.at[0, i], t_recv.at[0], x_peers[i]) for i in range(3)]
    lower_z = [remote(lower, lower, t_send.at[1, i], t_recv.at[1], z_peers[i]) for i in range(3)]
    upper_z = [remote(upper, upper, t_send.at[2, i], t_recv.at[0], z_peers[i]) for i in range(3)]
    lower_x = [remote(lower, lower, t_send.at[3, i], t_recv.at[1], x_peers[i]) for i in range(3)]
    own_square = remote(square.at[core], square.at[core], s_send.at[0], s_recv.at[0], sibling)

    start, end = pl.ds(0, PIECE // 2), pl.ds(PIECE // 2, PIECE // 2)
    scatter = [
        remote(
            raw_ref.at[i], panel.at[core, i // 4, i % 4, pl.ds(0, NB)], scatter_send.at[i - 1], scatter_recv.at[0],
            (p, column(i // 4, i % 4, core)),
        )
        for i in range(1, 16)
    ]
    scatter_lines = [
        remote(
            disp_buf.at[pl.ds(16 * i, 16)], panel.at[core, i // 4, i % 4, pl.ds(NB, 16)],
            scatter_send.at[14 + i], scatter_recv.at[1], (p, column(i // 4, i % 4, core)),
        )
        for i in range(1, 16)
    ]
    own_piece = pltpu.make_async_copy(raw_ref.at[0], panel.at[core, 0, 0, pl.ds(0, NB)], local_sem.at[0])
    own_lines = pltpu.make_async_copy(
        disp_buf.at[pl.ds(0, 16)], panel.at[core, 0, 0, pl.ds(NB, 16)], local_sem.at[6]
    )
    along = []
    for i in range(3):
        mine_low, mine_high = panel.at[core, cx, cz, start], panel.at[core, cx, cz, end]
        along.append(remote(mine_low, mine_low, x_send.at[0, i], x_recv.at[0, i], x_peers[i]))
        along.append(remote(mine_high, mine_high, z_send.at[0, i], z_recv.at[0, i], z_peers[i]))
    spread = []
    for i in range(3):
        mine_low, mine_high = panel.at[core, :, cz, start], panel.at[core, cx, :, end]
        spread.append(remote(mine_low, mine_low, z_send.at[1, i], z_recv.at[1, i], z_peers[i]))
        spread.append(remote(mine_high, mine_high, x_send.at[1, i], x_recv.at[1, i], x_peers[i]))
    pair = remote(panel.at[core], panel.at[core], pair_send.at[0], pair_recv.at[0], sibling)

    @pl.when(root)
    def _():
        for i in range(16):
            raw_ref[i] = whole[pl.ds(i * NB * lines, NB, lines), :]
        for copy in scatter:
            copy.start()
        own_piece.start()
        disp_buf[pl.ds(2 * SLOTS_D, 2 * NB - 2 * SLOTS_D), :] = jnp.zeros((2 * NB - 2 * SLOTS_D, NB), F32)
        own_arr.wait()
        for copy in arr_panel:
            copy.wait_recv()
        onehot = jnp.where(iota((2 * NB, 4 * SLOTS_A), 1) == slot_ref[:, :1], 1.0, 0.0).astype(BF16)
        square[core] = onehot_rows(onehot, arr_buf[...])
        for copy in upper_x + lower_z:
            copy.start()

    @pl.when(jnp.logical_not(root))
    def _():
        upper_x[0].wait_recv()

    @pl.when(cz == 0)
    def _():
        for copy in upper_z:
            copy.start()

    @pl.when(jnp.logical_not(root))
    def _():
        lower_z[0].wait_recv()

    @pl.when(cx == 0)
    def _():
        for copy in lower_x:
            copy.start()

    own_square.start()

    @pl.when(root)
    def _():
        for source in range(2):
            @pl.when(p == source)
            def _():
                own_disp.wait()

            @pl.when(p != source)
            def _(source=source):
                remote(disp_for(0), disp_lines(source), p_send.at[3], p_recv.at[3 + source], up).wait_recv()
        for copy in scatter_lines:
            copy.start()
        own_lines.start()

    own_square.wait_recv()
    a_ref[...] = square[...]
    t_ref[...] = jnp.zeros(t_ref.shape, F32)

    def pass_rows():
        bulk[0].wait_recv()
        forward[0].start()
        bulk[1].wait_recv()
        forward[1].start()

    def pass_piece():
        @pl.when(root)
        def _():
            own_piece.wait()
            own_lines.wait()

        @pl.when(jnp.logical_not(root))
        def _():
            scatter[0].wait_recv()
            scatter_lines[0].wait_recv()

        for copy in along:
            copy.start()

    def pass_pieces():
        for copy in along:
            copy.wait_recv()
        for copy in spread:
            copy.start()

    def pass_panel():
        for copy in spread:
            copy.wait_recv()
        pair.start()

    events = [{2: pass_piece, 3: pass_rows, 6: pass_pieces}, {6: pass_panel}]
    for half_number in range(2):
        def factor_step(index, carry, half_number=half_number):
            for when, event in events[half_number].items():
                pl.when(index == when)(event)
            eliminate(a_ref, xl_ref, xu_ref, t_ref, index, half_number)
            return carry

        lax.fori_loop(0, 8, factor_step, 0)
    packed, left, right = inverses(a_ref, xl_ref, xu_ref)
    packed_ref[...] = packed
    linv_ref[...] = left
    uinv_ref[...] = right

    bulk[2].wait_recv()
    bulk[3].wait_recv()
    for copy in forward:
        copy.wait_recv()
    own_rows.wait()
    for source in range(2):
        @pl.when(p == source)
        def _():
            own_moved.wait()

        @pl.when(p != source)
        def _(source=source):
            remote(moved_to(0), moved(source), y_send.at[4], y_recv.at[4 + source], up).wait_recv()
    pair.wait_recv()
    for copy in bulk + forward + along + spread + [pair]:
        copy.wait_send()

    @pl.when(p < 2)
    def _():
        to_up.wait_send()
        to_down.wait_send()
        to_across.wait_send()

    @pl.when(cz == 0)
    def _():
        for copy in upper_z:
            copy.wait_send()

    @pl.when(cx == 0)
    def _():
        for copy in lower_x:
            copy.wait_send()

    own_square.wait_send()

    @pl.when(root)
    def _():
        for copy in arr_panel + upper_x + lower_z + scatter + scatter_lines:
            copy.wait_send()

        @pl.when(p < 2)
        def _():
            for copy in disp_panel:
                copy.wait_send()


def front_call(idx, slot, x, lines):
    dma = pltpu.SemaphoreType.DMA
    vmem = pl.BlockSpec(memory_space=pltpu.VMEM)
    result = jax.ShapeDtypeStruct((2 * NB, 2 * NB), F32)
    sizes = [(4 * SLOTS_A * lines,), (2 * NB * lines,), (2, 4, 4, PIECE)]
    held = [
        x.shape[:1], (NB * lines,), (SLOTS_A * lines,), (4 * SLOTS_D * lines,), (SLOTS_A,), (4 * SLOTS_D,), (16, NB),
        (4 * SLOTS_A,), (2 * NB,), (2, 2 * NB), (2, 2 * NB), (2, 2 * NB), (2, 2 * NB), (2, NB),
    ]
    semaphores = [
        (LOADS,), (7,), (9,), (9,), (6,), (5,), (4, 3), (2,), (1,), (1,),
        (30,), (2,), (2, 3), (2, 3), (2, 3), (2, 3), (1,), (1,),
    ]
    return pl.pallas_call(
        front_kernel,
        in_specs=[pl.BlockSpec(memory_space=pltpu.SMEM), vmem, ANY],
        out_specs=[ANY] * 3 + [vmem] * 3,
        out_shape=[jax.ShapeDtypeStruct(size + (NB,), F32) for size in sizes] + [result] * 3,
        scratch_shapes=[pltpu.VMEM(size + (NB,), F32) for size in held] + [dma(shape) for shape in semaphores],
        compiler_params=pltpu.CompilerParams(
            collective_id=0, has_side_effects=True, vmem_limit_bytes=48 * 2**20
        ),
        name="front",
    )(idx, slot, x)


STEP_ROWS = 256


def update_kernel(
    idx_ref, x_ref, panel_ref, disp_in, arr_in, slot_ref, packed_ref, linv_ref, uinv_ref, o_ref,
    whole, pan, disp_ref, arr_ref, stacked, u_ref, done, x_sem, pan_sem, disp_sem, arr_sem,
):
    p = lax.axis_index("prow")
    q = lax.axis_index("pcol")
    step = pl.program_id(0)
    lines = whole.shape[0] // (16 * NB)
    size = STEP_ROWS * lines

    def load_x(number):
        here = pl.ds(pl.multiple_of(number * size, 8), size)
        return pltpu.make_async_copy(x_ref.at[here], whole.at[here], x_sem.at[number])

    @pl.when(step == 0)
    def _():
        loads = []
        part = 4 * SLOTS_A * lines // 4
        for number in range(4):
            here = pl.ds(number * part, part)
            loads.append(pltpu.make_async_copy(arr_in.at[here], arr_ref.at[here], arr_sem.at[number]))
        for half in range(2):
            loads.append(pltpu.make_async_copy(panel_ref.at[half], pan.at[half], pan_sem.at[half]))
            here = pl.ds(half * NB * lines, NB * lines)
            loads.append(pltpu.make_async_copy(disp_in.at[here], disp_ref.at[here], disp_sem.at[half]))
        for load in loads:
            load.start()
        for number in range(16 * NB // STEP_ROWS):
            load_x(number).start()
        done[0] = 0
        high, low = split(linv_ref[...])
        slot = slot_ref[:, :1]
        onehot = jnp.where(iota((2 * NB, 4 * SLOTS_A), 1) == slot, 1.0, 0.0).astype(BF16)
        left = (dot(high, onehot).astype(BF16), dot(low, onehot).astype(BF16))
        for load in loads[:4]:
            load.wait()
        for c in range(lines):
            rows = arr_ref[pl.ds(c, 4 * SLOTS_A, lines), :]
            value = dot3(left, split(rows))
            here = slice(c * NB, (c + 1) * NB)
            u_ref[:, here] = value
            upper, rest = split(value)
            stacked[0 : 2 * NB, here] = upper
            stacked[2 * NB : 4 * NB, here] = rest
            stacked[4 * NB : 6 * NB, here] = upper
        for load in loads[4:]:
            load.wait()

    load_x(step).wait()
    bound = (step + 1) * STEP_ROWS

    def more(t):
        return (t < idx_ref[IN_COUNT, 0]) & (idx_ref[IN_TARGET, jnp.minimum(t, 2 * NB - 1)] < bound)

    def patch(t):
        target = idx_ref[IN_TARGET, t]
        line = idx_ref[IN_LINE, t]
        panel_row = (target >> 7) * PIECE + (target & (NB - 1))
        for half in range(2):
            pan[half, pl.ds(panel_row, 1), :] = pan[half, pl.ds(line, 1), :]
        source = idx_ref[IN_ROW, t] * lines
        whole[pl.ds(target * lines, lines), :] = disp_ref[pl.ds(source, lines), :]
        return t + 1

    done[0] = lax.while_loop(more, patch, done[0])

    rows = []
    for number in range(STEP_ROWS // NB):
        here = pl.ds(pl.multiple_of((step * (STEP_ROWS // NB) + number) * PIECE, 8), NB)
        rows.append(jnp.concatenate([pan[0, here, :], pan[1, here, :]], 1))
    rows = jnp.concatenate(rows, 0)
    mult = dot3(split(rows), split(uinv_ref[...]))
    high, low = split(mult)
    left = jnp.concatenate([high, high, low], 1)
    base = step * (STEP_ROWS * lines)
    for c in range(0, lines, 2):
        product = dot(left, stacked[:, c * NB : (c + 2) * NB])
        for k in range(2):
            current = whole[pl.ds(base + c + k, STEP_ROWS, lines), :]
            o_ref[pl.ds(c + k, STEP_ROWS, lines), :] = current - product[:, k * NB : (k + 1) * NB]

    for half in range(2):
        @pl.when(q == half)
        def _(half=half):
            o_ref[pl.ds(0, STEP_ROWS, lines), :] = mult[:, half * NB : (half + 1) * NB]

    for half in range(2):
        @pl.when((p == half) & (step == 0))
        def _(half=half):
            top = slice(half * NB, (half + 1) * NB)
            for c in range(lines):
                value = u_ref[top, c * NB : (c + 1) * NB]
                if c == 0:
                    value = jnp.where(q == 0, packed_ref[top, :NB], jnp.where(q == 1, packed_ref[top, NB:], value))
                o_ref[pl.ds(c, NB, lines), :] = value


def update_call(idx, x, panel, disp, arr, slot, packed, linv, uinv, lines):
    vmem = pl.BlockSpec(memory_space=pltpu.VMEM)
    return pl.pallas_call(
        update_kernel,
        grid=(16 * NB // STEP_ROWS,),
        in_specs=[pl.BlockSpec(memory_space=pltpu.SMEM)] + [ANY] * 4 + [vmem] * 4,
        out_specs=pl.BlockSpec((STEP_ROWS * lines, NB), lambda i: (i, 0)),
        out_shape=jax.ShapeDtypeStruct((16 * NB * lines, NB), F32),
        scratch_shapes=[
            pltpu.VMEM((16 * NB * lines, NB), F32),
            pltpu.VMEM((2, 16 * PIECE, NB), F32),
            pltpu.VMEM((2 * NB * lines, NB), F32),
            pltpu.VMEM((4 * SLOTS_A * lines, NB), F32),
            pltpu.VMEM((6 * NB, NB * lines), BF16),
            pltpu.VMEM((2 * NB, NB * lines), F32),
            pltpu.SMEM((1,), jnp.int32),
            pltpu.SemaphoreType.DMA((16 * NB // STEP_ROWS,)),
            pltpu.SemaphoreType.DMA((2,)),
            pltpu.SemaphoreType.DMA((2,)),
            pltpu.SemaphoreType.DMA((4,)),
        ],
        compiler_params=pltpu.CompilerParams(vmem_limit_bytes=48 * 2**20),
        name="update",
    )(idx, x, panel, disp, arr, slot, packed, linv, uinv)


def shards(matrix, pivots):
    lines = matrix.shape[3]
    rows = matrix.shape[0] * NB
    p = lax.axis_index("prow")
    q = lax.axis_index("pcol")
    x = matrix.reshape(rows * lines, NB)
    idx, slot = index_call(pivots)

    def total(x, axis, count):
        bit = 1
        while bit < count:
            x = x + lax.ppermute(x, axis, [(i, i ^ bit) for i in range(count)])
            bit *= 2
        return x

    def fits(x, idx, slot):
        recv_arr, recv_disp, panel, packed, linv, uinv = front_call(idx, slot, x, lines)
        return recv_arr, recv_disp, panel, packed, linv, uinv, idx, slot

    def general(x, idx, slot):
        x = x.reshape(rows, lines, NB)
        chosen = jnp.where((idx[OWNER] == p)[:, None, None], jnp.take(x, idx[LOCAL], axis=0), 0.0)
        top = jnp.concatenate([jnp.where(p == s, x[:NB], 0.0) for s in range(2)])
        chosen, top = total(chosen, "prow", 4), total(top, "prow", 4)
        own = jnp.concatenate([x[:, 0].reshape(16, NB, NB), top[:, 0].reshape(16, 16, NB)], 1)
        own = jnp.concatenate([own.reshape(-1, NB), chosen[:, 0]])
        both = total(jnp.stack([jnp.where(q == s, own, 0.0) for s in range(2)]), "pcol", 32)
        panel = both[:, : 16 * PIECE].reshape(2, 4, 4, PIECE, NB)
        order = jnp.arange(2 * NB, dtype=jnp.int32)
        idx = idx.at[IN_ROW].set(idx[IN_ORIGIN]).at[IN_LINE].set(panel_line(idx[IN_ORIGIN]))
        slot = jnp.broadcast_to(order[:, None], slot.shape)
        packed, linv, uinv = lu_call(both[:, 16 * PIECE :])
        chosen = jnp.pad(chosen, ((0, 4 * SLOTS_A - 2 * NB), (0, 0), (0, 0)))
        return chosen.reshape(-1, NB), top.reshape(-1, NB), panel, packed, linv, uinv, idx, slot

    arr, disp, panel, packed, linv, uinv, idx, slot = lax.cond(idx[OVER, 0] == 0, fits, general, x, idx, slot)
    panel = panel.reshape(2, -1, NB)
    out = update_call(idx, x, panel, disp, arr, slot, packed, linv, uinv, lines)
    return out.reshape(matrix.shape)


def solution(mesh):
    placed = (P(None, "prow", None, None, "pcol", None), P())
    return jax.shard_map(
        shards,
        mesh=mesh,
        in_specs=placed,
        out_specs=P(None, "prow", None, None, "pcol", None),
        check_vma=False,
    )
```

```python
import jax
import jax.numpy as jnp
from jax import lax
from jax.experimental import pallas as pl
from jax.experimental.pallas import tpu as pltpu
from jax.sharding import PartitionSpec as P

NB = 128
F32 = jnp.float32
BF16 = jnp.bfloat16
MESH = pl.DeviceIdType.MESH
SLOTS_A = 88
SLOTS_D = 56
LOADS = 16
PIECE = NB + 16
(
    OWNER, LOCAL, OVER, ARR_LOCAL, OUT_LOCAL, IN_TARGET, IN_ROW, IN_LINE, IN_ORIGIN, IN_COUNT,
) = range(10)


def split(x):
    high = x.astype(BF16)
    return high, (x - high.astype(F32)).astype(BF16)


def dot(a, b):
    return jnp.dot(a, b, preferred_element_type=F32)


def dot3(a, b):
    ah, al = a
    bh, bl = b
    return dot(ah, bh) + (dot(ah, bl) + dot(al, bh))


def onehot_rows(onehot, x):
    high = x.astype(BF16)
    rest = x - high.astype(F32)
    mid = rest.astype(BF16)
    low = (rest - mid.astype(F32)).astype(BF16)
    return (dot(onehot, high) + dot(onehot, mid)) + dot(onehot, low)


def iota(shape, dim):
    return lax.broadcasted_iota(jnp.int32, shape, dim)


def eliminate(a_ref, xl_ref, xu_ref, t_ref, index, half):
    local = pl.multiple_of(index * 16, 16)
    start = pl.multiple_of(half * NB + local, 16)
    sub = iota((16, NB), 0)
    lane = iota((16, NB), 1)
    original = [a_ref[g, pl.ds(start, 16), :] for g in range(2)]
    rolled = pltpu.roll(original[half], lax.rem(NB - local, NB), axis=1)
    cols = [jnp.broadcast_to(rolled[:, j : j + 1], (16, NB)) for j in range(16)]
    upper = list(original[half:])
    jordan = list(original[half:])
    ident = jnp.where((lane == sub) | (lane == sub + 16), 1.0, 0.0).astype(F32)
    factors = jnp.zeros((16, NB), F32)
    scale = jnp.zeros((16, NB), F32)

    def pick(x, k):
        return jnp.broadcast_to(x[k : k + 1, :], (16, NB))

    for k in range(16):
        inverse = 1.0 / pick(cols[k], k)
        mult = cols[k] * inverse
        low = jnp.where(sub > k, mult, 0.0)
        both = jnp.where(sub != k, mult, 0.0)
        for j in range(k + 1, 16):
            cols[j] = cols[j] - both * pick(cols[j], k)
        upper = [x - low * pick(x, k) for x in upper]
        jordan = [x - both * pick(x, k) for x in jordan]
        mixed = jnp.where(lane < 16, low, both - low)
        ident = ident - mixed * pick(ident, k)
        factors = jnp.where((lane == local + k) & (sub > k), mult, factors)
        scale = jnp.where(sub == k, inverse, scale)

    in_block = (lane >= local) & (lane < local + 16)
    lower_of_block = in_block & (lane - local < sub)
    merged = jnp.where(lower_of_block, factors, jnp.where(lane < local, original[half], upper[0]))
    a_ref[half, pl.ds(start, 16), :] = merged
    if half == 0:
        a_ref[1, pl.ds(start, 16), :] = upper[1]
    left_inv = pltpu.roll(jnp.where(lane < 16, ident, 0.0), local, axis=1)
    right_inv = pltpu.roll(
        jnp.where((lane >= 16) & (lane < 32), ident * scale, 0.0), lax.rem(local + NB - 16, NB), axis=1
    )
    zero = jnp.zeros((16, NB), F32)
    xl_ref[half, pl.ds(start, 16), :] = left_inv
    xl_ref[1 - half, pl.ds(start, 16), :] = zero
    xu_ref[half, pl.ds(start, 16), :] = right_inv
    xu_ref[1 - half, pl.ds(start, 16), :] = zero

    t_ref[0, pl.ds(local, 16), :] = jnp.where(
        lane >= local + 16, jordan[0] * scale, jnp.where(in_block, right_inv, 0.0)
    )
    if half == 0:
        t_ref[1, pl.ds(local, 16), :] = jordan[1] * scale
    rows = 2 * NB - half * NB
    below = iota((rows, NB), 0) + half * NB >= start + 16
    wide_lane = iota((rows, NB), 1)
    block_lane = (wide_lane >= local) & (wide_lane < local + 16)
    panel = a_ref[half, half * NB :, :]
    panel_parts = split(panel)
    product = dot3(panel_parts, split(t_ref[0]))
    a_ref[half, half * NB :, :] = jnp.where(
        below, jnp.where(block_lane, product, panel - product), panel
    )
    if half == 0:
        other = a_ref[1]
        product = dot3(panel_parts, split(t_ref[1]))
        a_ref[1] = jnp.where(below, other - product, other)
    t_ref[0, pl.ds(local, 16), :] = zero
    if half == 0:
        t_ref[1, pl.ds(local, 16), :] = zero


def inverses(a_ref, xl_ref, xu_ref):
    packed = jnp.concatenate([a_ref[0], a_ref[1]], 1)
    left = jnp.concatenate([xl_ref[0], xl_ref[1]], 1)
    right = jnp.concatenate([xu_ref[0], xu_ref[1]], 1)
    row = iota((256, 256), 0)
    col = iota((256, 256), 1)
    size = 16
    while size < 256:
        pair = row // (2 * size) == col // (2 * size)
        low_corner = pair & (row % (2 * size) >= size) & (col % (2 * size) < size)
        up_corner = pair & (row % (2 * size) < size) & (col % (2 * size) >= size)
        left_parts = split(left)
        right_parts = split(right)
        first = dot3(left_parts, split(jnp.where(low_corner, packed, 0.0)))
        second = dot3(right_parts, split(jnp.where(up_corner, packed, 0.0)))
        left = left - dot3(split(first), left_parts)
        right = right - dot3(split(second), right_parts)
        size *= 2
    return packed, left, right


def lu_kernel(square_ref, packed_ref, linv_ref, uinv_ref, a_ref, xl_ref, xu_ref, t_ref):
    a_ref[...] = square_ref[...]
    t_ref[...] = jnp.zeros(t_ref.shape, F32)
    for half in range(2):
        def step(index, carry, half=half):
            eliminate(a_ref, xl_ref, xu_ref, t_ref, index, half)
            return carry

        lax.fori_loop(0, 8, step, 0)
    packed, left, right = inverses(a_ref, xl_ref, xu_ref)
    packed_ref[...] = packed
    linv_ref[...] = left
    uinv_ref[...] = right


def lu_call(square):
    result = jax.ShapeDtypeStruct((2 * NB, 2 * NB), F32)
    return pl.pallas_call(
        lu_kernel,
        out_shape=[result] * 3,
        scratch_shapes=[pltpu.VMEM((2, 2 * NB, NB), F32)] * 3 + [pltpu.VMEM((2, NB, NB), F32)],
        compiler_params=pltpu.CompilerParams(vmem_limit_bytes=32 * 2**20),
        name="factor",
    )(square)


def panel_line(number):
    return (number >> 4) * PIECE + NB + (number & 15)


def index_kernel(piv_ref, idx_ref, slot_ref):
    lane = iota((NB, NB), 1).astype(F32)
    sub = iota((NB, NB), 0).astype(F32)

    def rows(x):
        return jnp.broadcast_to(x, (NB, NB))

    def lanes_sum(cond, value=1.0):
        return rows(jnp.sum(jnp.where(cond, value, 0.0), axis=1, keepdims=True))

    def subs_sum(cond, value=1.0):
        return rows(jnp.sum(jnp.where(cond, value, 0.0), axis=0, keepdims=True))

    given = piv_ref[...].astype(F32)
    row = [rows(given[s : s + 1, :]) for s in range(2)]
    col = [x.T for x in row]
    fill_row, fill_col = [], []
    for s in range(2):
        start = float(s * NB)
        listed_row = subs_sum(col[s] == lane + start)
        listed_col = lanes_sum(row[s] == sub + start)
        rank_vacated = lanes_sum((lane <= sub) & (row[s] >= start + NB))
        rank_displaced = subs_sum((sub <= lane) & (listed_col == 0.0))
        pairing = (col[s] >= start + NB) & (listed_row == 0.0) & (rank_vacated == rank_displaced)
        filler = lanes_sum(pairing, lane + start)
        fill_col.append(filler)
        fill_row.append(filler.T)
    again = col[1] == row[0]
    source_col = jnp.where(lanes_sum(again) > 0.0, lanes_sum(again, fill_row[0]), col[1])
    moved = fill_col[1] == row[0]
    second_col = jnp.where(lanes_sum(moved) > 0.0, lanes_sum(moved, fill_row[0]), fill_col[1])

    def whole(x):
        return x.astype(jnp.int32)

    def place(value):
        number = whole(value)
        return (number >> 7) & 3, (number >> 9) * NB + (number & (NB - 1))

    def ranks(keys):
        keys_row = [k.astype(F32) for k in keys]
        keys_col = [k.T for k in keys_row]
        first = subs_sum((keys_col[0] == keys_row[0]) & (sub < lane))
        second = subs_sum((keys_col[1] == keys_row[1]) & (sub < lane)) + subs_sum(
            keys_col[0] == keys_row[1]
        )
        return [whole(first), whole(second)]

    sources = [row[0], source_col.T]
    owners, locals_ = zip(*[place(x) for x in sources])
    rank_arr = ranks(owners)
    slots = [o * SLOTS_A + r for o, r in zip(owners, rank_arr)]
    valid = [(row[0] >= 2.0 * NB) & (subs_sum(again) == 0.0), row[1] >= 2.0 * NB]
    origins = [whole(fill_row[0]), whole(second_col.T)]
    dests, targets = zip(*[place(x) for x in row])
    halves = [x >> 7 for x in origins]
    keys = [jnp.where(v, h * 4 + d, 9) for v, h, d in zip(valid, halves, dests)]
    rank_disp = ranks(keys)
    zero = jnp.zeros((NB, NB), jnp.int32)
    over = zero
    for g in range(2):
        over = over + whole(rows(jnp.sum(jnp.where(rank_arr[g] >= SLOTS_A, 1.0, 0.0), axis=1, keepdims=True)))
        bad = valid[g] & (rank_disp[g] >= SLOTS_D)
        over = over + whole(rows(jnp.sum(jnp.where(bad, 1.0, 0.0), axis=1, keepdims=True)))
    me = lax.axis_index("prow")

    def compact(chosen, values, keys):
        chosen = [jnp.where(c, 1.0, 0.0) for c in chosen]
        chosen_col = [c.T for c in chosen]
        keys_col = [k.T for k in keys]
        before = [
            sum(subs_sum((c > 0.0) & (k < key)) for c, k in zip(chosen_col, keys_col)) for key in keys
        ]
        total = sum(subs_sum(c > 0.0) for c in chosen_col)
        order = [jnp.where(c > 0.0, r, -1.0).T for c, r in zip(chosen, before)]
        packed = []
        for value in values:
            value_col = [v.astype(F32).T for v in value]
            packed.append(
                [
                    whole(sum(subs_sum(o == lane + g * NB, v) for o, v in zip(order, value_col)))
                    for g in range(2)
                ]
            )
        count = whole(total)
        return packed, [count, count]

    (arr_local,), _ = compact([o == me for o in owners], [locals_], [lane, lane + NB])
    out_slot = [
        jnp.where(v & (h == me), d * SLOTS_D + r, -1).astype(F32).T
        for v, h, d, r in zip(valid, halves, dests, rank_disp)
    ]
    out_row = [(x & (NB - 1)).astype(F32).T for x in origins]
    out_local = [
        whole(sum(subs_sum(o == lane + g * NB, v) for o, v in zip(out_slot, out_row))) for g in range(2)
    ]
    (in_target, in_row, in_line, in_origin), in_count = compact(
        [v & (d == me) for v, d in zip(valid, dests)],
        [
            targets,
            [h * NB + r for h, r in zip(halves, rank_disp)],
            [panel_line(h * SLOTS_D + r) for h, r in zip(halves, rank_disp)],
            origins,
        ],
        [t.astype(F32) for t in targets],
    )
    fields = [
        owners, locals_, [over, over], arr_local, out_local,
        in_target, in_row, in_line, in_origin, in_count,
    ]
    for number, field in enumerate(fields):
        for g in range(2):
            idx_ref[number : number + 1, g * NB : (g + 1) * NB] = field[g][0:1, :]
    for number in range(len(fields), 16):
        idx_ref[number : number + 1, :] = jnp.zeros((1, 2 * NB), jnp.int32)
    for g in range(2):
        slot_ref[g * NB : (g + 1) * NB, :] = whole(slots[g].astype(F32).T)


def index_call(pivots):
    return pl.pallas_call(
        index_kernel,
        out_shape=[
            jax.ShapeDtypeStruct((16, 2 * NB), jnp.int32),
            jax.ShapeDtypeStruct((2 * NB, NB), jnp.int32),
        ],
        name="indices",
    )(pivots)


ANY = pl.BlockSpec(memory_space=pl.ANY)


def rows8(start, size):
    return pl.ds(pl.multiple_of(start, 8), size)


def front_kernel(
    idx_ref, slot_ref, x_ref, recv_arr, recv_disp, panel, packed_ref, linv_ref, uinv_ref,
    whole, top, arr_ref, disp_ref, arr_line_ref, disp_line_ref, raw_ref, arr_buf, disp_buf, square,
    a_ref, xl_ref, xu_ref, t_ref,
    load_sem, local_sem, y_send, y_recv, p_send, p_recv, t_send, t_recv, s_send, s_recv,
    scatter_send, scatter_recv, x_send, x_recv, z_send, z_recv, pair_send, pair_recv,
):
    lines = whole.shape[0] // (16 * NB)
    size = whole.shape[0] // LOADS
    load_top = pltpu.make_async_copy(x_ref.at[pl.ds(0, NB * lines)], top, local_sem.at[5])
    load_top.start()
    loads = []
    for number in range(LOADS):
        here = pl.ds(number * size, size)
        loads.append(pltpu.make_async_copy(x_ref.at[here], whole.at[here], load_sem.at[number]))
        loads[-1].start()
    p = lax.axis_index("prow")
    q = lax.axis_index("pcol")
    cx, cz, core = q // 8, (q // 2) % 4, q % 2
    root = q < 2

    def column(ix, iz, icore):
        return (ix % 4 * 4 + iz % 4) * 2 + icore

    up, down, across = ((p + 1) % 4, q), ((p + 3) % 4, q), ((p + 2) % 4, q)
    sibling = (p, column(cx, cz, 1 - core))
    x_peers = [(p, column(cx + i, cz, core)) for i in (1, 2, 3)]
    z_peers = [(p, column(cx, cz + i, core)) for i in (1, 2, 3)]
    near = [up, down, across, sibling] + x_peers + z_peers
    barrier = pltpu.get_barrier_semaphore()
    for other in near:
        pl.semaphore_signal(barrier, inc=1, device_id=other, device_id_type=MESH)

    @pl.when((cx > 0) & (cz > 0))
    def _():
        pl.semaphore_signal(barrier, inc=1, device_id=(p, core), device_id_type=MESH)

    def remote(src, dst, send, recv, device):
        return pltpu.make_async_remote_copy(
            src_ref=src, dst_ref=dst, send_sem=send, recv_sem=recv, device_id=device, device_id_type=MESH
        )

    load_top.wait()

    def displaced(t, carry):
        disp_ref[pl.ds(t * lines, lines), :] = top[pl.ds(idx_ref[OUT_LOCAL, t] * lines, lines), :]
        return carry

    def arriving(j, carry):
        arr_ref[pl.ds(j * lines, lines), :] = whole[pl.ds(idx_ref[ARR_LOCAL, j] * lines, lines), :]
        return carry

    @pl.when(p < 2)
    def _():
        lax.fori_loop(0, 4 * SLOTS_D, displaced, 0, unroll=4)
        disp_line_ref[...] = disp_ref[pl.ds(0, 4 * SLOTS_D, lines), :]

    pl.semaphore_wait(barrier, jnp.where(root, len(near) + 9, len(near)))

    def arr_lines(owner):
        return arr_buf.at[rows8(owner * SLOTS_A, SLOTS_A)]

    def disp_lines(half):
        return disp_buf.at[rows8(half * SLOTS_D, SLOTS_D)]

    def disp_for(owner):
        return disp_line_ref.at[rows8(owner * SLOTS_D, SLOTS_D)]

    peers = [up, down, across]
    own_arr = pltpu.make_async_copy(arr_line_ref, arr_lines(p), local_sem.at[1])
    own_disp = pltpu.make_async_copy(disp_for(p), disp_lines(p % 2), local_sem.at[2])
    arr_panel = [remote(arr_line_ref, arr_lines(p), p_send.at[i], p_recv.at[i], peers[i]) for i in range(3)]
    disp_panel = [
        remote(disp_for(peers[i][0]), disp_lines(p % 2), p_send.at[3 + i], p_recv.at[3 + p % 2], peers[i])
        for i in range(3)
    ]

    @pl.when(root & (p < 2))
    def _():
        for copy in disp_panel:
            copy.start()
        own_disp.start()

    arr_size, disp_size = arr_ref.shape[0], disp_ref.shape[0] // 4
    half_size = arr_size // 2
    low, high = pl.ds(0, half_size), pl.ds(half_size, half_size)

    def arr_rows(owner, part):
        return recv_arr.at[rows8(owner * arr_size + part.start, part.size)]

    def moved_to(owner):
        return disp_ref.at[rows8(owner * disp_size, disp_size)]

    def moved(half):
        return recv_disp.at[rows8(half * (recv_disp.shape[0] // 2), disp_size)]

    own_rows = pltpu.make_async_copy(arr_ref, recv_arr.at[rows8(p * arr_size, arr_size)], local_sem.at[3])
    own_moved = pltpu.make_async_copy(moved_to(p), moved(p % 2), local_sem.at[4])
    bulk = [
        remote(arr_ref.at[low], arr_rows(p, low), y_send.at[0], y_recv.at[0], up),
        remote(arr_ref.at[high], arr_rows(p, high), y_send.at[1], y_recv.at[1], down),
        remote(arr_ref.at[high], arr_rows(p, high), y_send.at[2], y_recv.at[2], up),
        remote(arr_ref.at[low], arr_rows(p, low), y_send.at[3], y_recv.at[3], down),
    ]
    half = p % 2
    to_up = remote(moved_to(up[0]), moved(half), y_send.at[4], y_recv.at[4 + half], up)
    to_down = remote(moved_to(down[0]), moved(half), y_send.at[5], y_recv.at[4 + half], down)
    to_across = remote(moved_to(across[0]), moved(half), y_send.at[6], y_recv.at[4 + half], across)

    @pl.when(p < 2)
    def _():
        to_across.start()
        own_moved.start()

    forward = [
        remote(arr_rows(down[0], low), arr_rows(down[0], low), y_send.at[7], y_recv.at[7], up),
        remote(arr_rows(up[0], high), arr_rows(up[0], high), y_send.at[8], y_recv.at[8], down),
    ]
    for load in loads:
        load.wait()
    lax.fori_loop(0, SLOTS_A, arriving, 0, unroll=4)
    arr_line_ref[...] = arr_ref[pl.ds(0, SLOTS_A, lines), :]

    @pl.when(root)
    def _():
        for copy in arr_panel:
            copy.start()
        own_arr.start()

    for copy in bulk:
        copy.start()
    own_rows.start()

    @pl.when(p < 2)
    def _():
        to_up.start()
        to_down.start()

    upper, lower = square.at[core, pl.ds(0, NB)], square.at[core, pl.ds(NB, NB)]
    upper_x = [remote(upper, upper, t_send.at[0, i], t_recv.at[0], x_peers[i]) for i in range(3)]
    lower_z = [remote(lower, lower, t_send.at[1, i], t_recv.at[1], z_peers[i]) for i in range(3)]
    upper_z = [remote(upper, upper, t_send.at[2, i], t_recv.at[0], z_peers[i]) for i in range(3)]
    lower_x = [remote(lower, lower, t_send.at[3, i], t_recv.at[1], x_peers[i]) for i in range(3)]
    own_square = remote(square.at[core], square.at[core], s_send.at[0], s_recv.at[0], sibling)

    start, end = pl.ds(0, PIECE // 2), pl.ds(PIECE // 2, PIECE // 2)
    scatter = [
        remote(
            raw_ref.at[i], panel.at[core, i // 4, i % 4, pl.ds(0, NB)], scatter_send.at[i - 1], scatter_recv.at[0],
            (p, column(i // 4, i % 4, core)),
        )
        for i in range(1, 16)
    ]
    scatter_lines = [
        remote(
            disp_buf.at[pl.ds(16 * i, 16)], panel.at[core, i // 4, i % 4, pl.ds(NB, 16)],
            scatter_send.at[14 + i], scatter_recv.at[1], (p, column(i // 4, i % 4, core)),
        )
        for i in range(1, 16)
    ]
    own_piece = pltpu.make_async_copy(raw_ref.at[0], panel.at[core, 0, 0, pl.ds(0, NB)], local_sem.at[0])
    own_lines = pltpu.make_async_copy(
        disp_buf.at[pl.ds(0, 16)], panel.at[core, 0, 0, pl.ds(NB, 16)], local_sem.at[6]
    )
    along = []
    for i in range(3):
        mine_low, mine_high = panel.at[core, cx, cz, start], panel.at[core, cx, cz, end]
        along.append(remote(mine_low, mine_low, x_send.at[0, i], x_recv.at[0, i], x_peers[i]))
        along.append(remote(mine_high, mine_high, z_send.at[0, i], z_recv.at[0, i], z_peers[i]))
    spread = []
    for i in range(3):
        mine_low, mine_high = panel.at[core, :, cz, start], panel.at[core, cx, :, end]
        spread.append(remote(mine_low, mine_low, z_send.at[1, i], z_recv.at[1, i], z_peers[i]))
        spread.append(remote(mine_high, mine_high, x_send.at[1, i], x_recv.at[1, i], x_peers[i]))
    pair = remote(panel.at[core], panel.at[core], pair_send.at[0], pair_recv.at[0], sibling)

    @pl.when(root)
    def _():
        for i in range(16):
            raw_ref[i] = whole[pl.ds(i * NB * lines, NB, lines), :]
        for copy in scatter:
            copy.start()
        own_piece.start()
        disp_buf[pl.ds(2 * SLOTS_D, 2 * NB - 2 * SLOTS_D), :] = jnp.zeros((2 * NB - 2 * SLOTS_D, NB), F32)
        own_arr.wait()
        for copy in arr_panel:
            copy.wait_recv()
        onehot = jnp.where(iota((2 * NB, 4 * SLOTS_A), 1) == slot_ref[:, :1], 1.0, 0.0).astype(BF16)
        square[core] = onehot_rows(onehot, arr_buf[...])
        for copy in upper_x + lower_z:
            copy.start()

    @pl.when(jnp.logical_not(root))
    def _():
        upper_x[0].wait_recv()

    @pl.when(cz == 0)
    def _():
        for copy in upper_z:
            copy.start()

    @pl.when(jnp.logical_not(root))
    def _():
        lower_z[0].wait_recv()

    @pl.when(cx == 0)
    def _():
        for copy in lower_x:
            copy.start()

    own_square.start()

    @pl.when(root)
    def _():
        for source in range(2):
            @pl.when(p == source)
            def _():
                own_disp.wait()

            @pl.when(p != source)
            def _(source=source):
                remote(disp_for(0), disp_lines(source), p_send.at[3], p_recv.at[3 + source], up).wait_recv()
        for copy in scatter_lines:
            copy.start()
        own_lines.start()

    own_square.wait_recv()
    a_ref[...] = square[...]
    t_ref[...] = jnp.zeros(t_ref.shape, F32)

    def pass_rows():
        bulk[0].wait_recv()
        forward[0].start()
        bulk[1].wait_recv()
        forward[1].start()

    def pass_piece():
        @pl.when(root)
        def _():
            own_piece.wait()
            own_lines.wait()

        @pl.when(jnp.logical_not(root))
        def _():
            scatter[0].wait_recv()
            scatter_lines[0].wait_recv()

        for copy in along:
            copy.start()

    def pass_pieces():
        for copy in along:
            copy.wait_recv()
        for copy in spread:
            copy.start()

    def pass_panel():
        for copy in spread:
            copy.wait_recv()
        pair.start()

    events = [{3: pass_piece, 5: pass_rows}, {0: pass_pieces, 7: pass_panel}]
    for half_number in range(2):
        def factor_step(index, carry, half_number=half_number):
            for when, event in events[half_number].items():
                pl.when(index == when)(event)
            eliminate(a_ref, xl_ref, xu_ref, t_ref, index, half_number)
            return carry

        lax.fori_loop(0, 8, factor_step, 0)
    packed, left, right = inverses(a_ref, xl_ref, xu_ref)
    packed_ref[...] = packed
    linv_ref[...] = left
    uinv_ref[...] = right

    bulk[2].wait_recv()
    bulk[3].wait_recv()
    for copy in forward:
        copy.wait_recv()
    own_rows.wait()
    for source in range(2):
        @pl.when(p == source)
        def _():
            own_moved.wait()

        @pl.when(p != source)
        def _(source=source):
            remote(moved_to(0), moved(source), y_send.at[4], y_recv.at[4 + source], up).wait_recv()
    pair.wait_recv()
    for copy in bulk + forward + along + spread + [pair]:
        copy.wait_send()

    @pl.when(p < 2)
    def _():
        to_up.wait_send()
        to_down.wait_send()
        to_across.wait_send()

    @pl.when(cz == 0)
    def _():
        for copy in upper_z:
            copy.wait_send()

    @pl.when(cx == 0)
    def _():
        for copy in lower_x:
            copy.wait_send()

    own_square.wait_send()

    @pl.when(root)
    def _():
        for copy in arr_panel + upper_x + lower_z + scatter + scatter_lines:
            copy.wait_send()

        @pl.when(p < 2)
        def _():
            for copy in disp_panel:
                copy.wait_send()


def front_call(idx, slot, x, lines):
    dma = pltpu.SemaphoreType.DMA
    vmem = pl.BlockSpec(memory_space=pltpu.VMEM)
    result = jax.ShapeDtypeStruct((2 * NB, 2 * NB), F32)
    sizes = [(4 * SLOTS_A * lines,), (2 * NB * lines,), (2, 4, 4, PIECE)]
    held = [
        x.shape[:1], (NB * lines,), (SLOTS_A * lines,), (4 * SLOTS_D * lines,), (SLOTS_A,), (4 * SLOTS_D,), (16, NB),
        (4 * SLOTS_A,), (2 * NB,), (2, 2 * NB), (2, 2 * NB), (2, 2 * NB), (2, 2 * NB), (2, NB),
    ]
    semaphores = [
        (LOADS,), (7,), (9,), (9,), (6,), (5,), (4, 3), (2,), (1,), (1,),
        (30,), (2,), (2, 3), (2, 3), (2, 3), (2, 3), (1,), (1,),
    ]
    return pl.pallas_call(
        front_kernel,
        in_specs=[pl.BlockSpec(memory_space=pltpu.SMEM), vmem, ANY],
        out_specs=[ANY] * 3 + [vmem] * 3,
        out_shape=[jax.ShapeDtypeStruct(size + (NB,), F32) for size in sizes] + [result] * 3,
        scratch_shapes=[pltpu.VMEM(size + (NB,), F32) for size in held] + [dma(shape) for shape in semaphores],
        compiler_params=pltpu.CompilerParams(
            collective_id=0, has_side_effects=True, vmem_limit_bytes=48 * 2**20
        ),
        name="front",
    )(idx, slot, x)


STEP_ROWS = 512
AHEAD = 2


def update_kernel(
    idx_ref, x_ref, panel_ref, disp_in, arr_in, slot_ref, packed_ref, linv_ref, uinv_ref, o_ref,
    whole, pan, disp_ref, arr_ref, stacked, u_ref, done, x_sem, pan_sem, disp_sem, arr_sem,
):
    p = lax.axis_index("prow")
    q = lax.axis_index("pcol")
    step = pl.program_id(0)
    lines = whole.shape[0] // (16 * NB)
    size = STEP_ROWS * lines

    def load_x(number):
        here = pl.ds(pl.multiple_of(number * size, 8), size)
        return pltpu.make_async_copy(x_ref.at[here], whole.at[here], x_sem.at[number])

    @pl.when(step == 0)
    def _():
        loads = []
        part = 4 * SLOTS_A * lines // 4
        for number in range(4):
            here = pl.ds(number * part, part)
            loads.append(pltpu.make_async_copy(arr_in.at[here], arr_ref.at[here], arr_sem.at[number]))
        for half in range(2):
            loads.append(pltpu.make_async_copy(panel_ref.at[half], pan.at[half], pan_sem.at[half]))
            here = pl.ds(half * NB * lines, NB * lines)
            loads.append(pltpu.make_async_copy(disp_in.at[here], disp_ref.at[here], disp_sem.at[half]))
        for load in loads:
            load.start()
        done[0] = 0
        high, low = split(linv_ref[...])
        slot = slot_ref[:, :1]
        onehot = jnp.where(iota((2 * NB, 4 * SLOTS_A), 1) == slot, 1.0, 0.0).astype(BF16)
        left = (dot(high, onehot).astype(BF16), dot(low, onehot).astype(BF16))
        for load in loads[:4]:
            load.wait()
        for number in range(AHEAD):
            load_x(number).start()
        for c in range(lines):
            rows = arr_ref[pl.ds(c, 4 * SLOTS_A, lines), :]
            value = dot3(left, split(rows))
            here = slice(c * NB, (c + 1) * NB)
            u_ref[:, here] = value
            upper, rest = split(value)
            stacked[0 : 2 * NB, here] = upper
            stacked[2 * NB : 4 * NB, here] = rest
            stacked[4 * NB : 6 * NB, here] = upper
        for load in loads[4:]:
            load.wait()

    @pl.when(step + AHEAD < 16 * NB // STEP_ROWS)
    def _():
        load_x(step + AHEAD).start()

    load_x(step).wait()
    bound = (step + 1) * STEP_ROWS

    def more(t):
        return (t < idx_ref[IN_COUNT, 0]) & (idx_ref[IN_TARGET, jnp.minimum(t, 2 * NB - 1)] < bound)

    def patch(t):
        target = idx_ref[IN_TARGET, t]
        line = idx_ref[IN_LINE, t]
        panel_row = (target >> 7) * PIECE + (target & (NB - 1))
        for half in range(2):
            pan[half, pl.ds(panel_row, 1), :] = pan[half, pl.ds(line, 1), :]
        source = idx_ref[IN_ROW, t] * lines
        whole[pl.ds(target * lines, lines), :] = disp_ref[pl.ds(source, lines), :]
        return t + 1

    done[0] = lax.while_loop(more, patch, done[0])

    rows = []
    for number in range(STEP_ROWS // NB):
        here = pl.ds(pl.multiple_of((step * (STEP_ROWS // NB) + number) * PIECE, 8), NB)
        rows.append(jnp.concatenate([pan[0, here, :], pan[1, here, :]], 1))
    rows = jnp.concatenate(rows, 0)
    mult = dot3(split(rows), split(uinv_ref[...]))
    high, low = split(mult)
    left = jnp.concatenate([high, high, low], 1)
    base = step * (STEP_ROWS * lines)
    for c in range(0, lines, 2):
        product = dot(left, stacked[:, c * NB : (c + 2) * NB])
        for k in range(2):
            current = whole[pl.ds(base + c + k, STEP_ROWS, lines), :]
            o_ref[pl.ds(c + k, STEP_ROWS, lines), :] = current - product[:, k * NB : (k + 1) * NB]

    for half in range(2):
        @pl.when(q == half)
        def _(half=half):
            o_ref[pl.ds(0, STEP_ROWS, lines), :] = mult[:, half * NB : (half + 1) * NB]

    for half in range(2):
        @pl.when((p == half) & (step == 0))
        def _(half=half):
            top = slice(half * NB, (half + 1) * NB)
            for c in range(lines):
                value = u_ref[top, c * NB : (c + 1) * NB]
                if c == 0:
                    value = jnp.where(q == 0, packed_ref[top, :NB], jnp.where(q == 1, packed_ref[top, NB:], value))
                o_ref[pl.ds(c, NB, lines), :] = value


def update_call(idx, x, panel, disp, arr, slot, packed, linv, uinv, lines):
    vmem = pl.BlockSpec(memory_space=pltpu.VMEM)
    return pl.pallas_call(
        update_kernel,
        grid=(16 * NB // STEP_ROWS,),
        in_specs=[pl.BlockSpec(memory_space=pltpu.SMEM)] + [ANY] * 4 + [vmem] * 4,
        out_specs=pl.BlockSpec((STEP_ROWS * lines, NB), lambda i: (i, 0)),
        out_shape=jax.ShapeDtypeStruct((16 * NB * lines, NB), F32),
        scratch_shapes=[
            pltpu.VMEM((16 * NB * lines, NB), F32),
            pltpu.VMEM((2, 16 * PIECE, NB), F32),
            pltpu.VMEM((2 * NB * lines, NB), F32),
            pltpu.VMEM((4 * SLOTS_A * lines, NB), F32),
            pltpu.VMEM((6 * NB, NB * lines), BF16),
            pltpu.VMEM((2 * NB, NB * lines), F32),
            pltpu.SMEM((1,), jnp.int32),
            pltpu.SemaphoreType.DMA((16 * NB // STEP_ROWS,)),
            pltpu.SemaphoreType.DMA((2,)),
            pltpu.SemaphoreType.DMA((2,)),
            pltpu.SemaphoreType.DMA((4,)),
        ],
        compiler_params=pltpu.CompilerParams(vmem_limit_bytes=48 * 2**20),
        name="update",
    )(idx, x, panel, disp, arr, slot, packed, linv, uinv)


def shards(matrix, pivots):
    lines = matrix.shape[3]
    rows = matrix.shape[0] * NB
    p = lax.axis_index("prow")
    q = lax.axis_index("pcol")
    x = matrix.reshape(rows * lines, NB)
    idx, slot = index_call(pivots)

    def total(x, axis, count):
        bit = 1
        while bit < count:
            x = x + lax.ppermute(x, axis, [(i, i ^ bit) for i in range(count)])
            bit *= 2
        return x

    def fits(x, idx, slot):
        recv_arr, recv_disp, panel, packed, linv, uinv = front_call(idx, slot, x, lines)
        return recv_arr, recv_disp, panel, packed, linv, uinv, idx, slot

    def general(x, idx, slot):
        x = x.reshape(rows, lines, NB)
        chosen = jnp.where((idx[OWNER] == p)[:, None, None], jnp.take(x, idx[LOCAL], axis=0), 0.0)
        top = jnp.concatenate([jnp.where(p == s, x[:NB], 0.0) for s in range(2)])
        chosen, top = total(chosen, "prow", 4), total(top, "prow", 4)
        own = jnp.concatenate([x[:, 0].reshape(16, NB, NB), top[:, 0].reshape(16, 16, NB)], 1)
        own = jnp.concatenate([own.reshape(-1, NB), chosen[:, 0]])
        both = total(jnp.stack([jnp.where(q == s, own, 0.0) for s in range(2)]), "pcol", 32)
        panel = both[:, : 16 * PIECE].reshape(2, 4, 4, PIECE, NB)
        order = jnp.arange(2 * NB, dtype=jnp.int32)
        idx = idx.at[IN_ROW].set(idx[IN_ORIGIN]).at[IN_LINE].set(panel_line(idx[IN_ORIGIN]))
        slot = jnp.broadcast_to(order[:, None], slot.shape)
        packed, linv, uinv = lu_call(both[:, 16 * PIECE :])
        chosen = jnp.pad(chosen, ((0, 4 * SLOTS_A - 2 * NB), (0, 0), (0, 0)))
        return chosen.reshape(-1, NB), top.reshape(-1, NB), panel, packed, linv, uinv, idx, slot

    arr, disp, panel, packed, linv, uinv, idx, slot = lax.cond(idx[OVER, 0] == 0, fits, general, x, idx, slot)
    panel = panel.reshape(2, -1, NB)
    out = update_call(idx, x, panel, disp, arr, slot, packed, linv, uinv, lines)
    return out.reshape(matrix.shape)


def solution(mesh):
    placed = (P(None, "prow", None, None, "pcol", None), P())
    return jax.shard_map(
        shards,
        mesh=mesh,
        in_specs=placed,
        out_specs=P(None, "prow", None, None, "pcol", None),
        check_vma=False,
    )
```

```python
import jax
import jax.numpy as jnp
from jax import lax
from jax.experimental import pallas as pl
from jax.experimental.pallas import tpu as pltpu
from jax.sharding import PartitionSpec as P

NB = 128
F32 = jnp.float32
BF16 = jnp.bfloat16
MESH = pl.DeviceIdType.MESH
SLOTS_A = 88
SLOTS_D = 56
LOADS = 16
PIECE = NB + 16
(
    OWNER, LOCAL, OVER, ARR_LOCAL, OUT_LOCAL, IN_TARGET, IN_ROW, IN_LINE, IN_ORIGIN, IN_COUNT,
) = range(10)


def split(x):
    high = x.astype(BF16)
    return high, (x - high.astype(F32)).astype(BF16)


def dot(a, b):
    return jnp.dot(a, b, preferred_element_type=F32)


def dot3(a, b):
    ah, al = a
    bh, bl = b
    return dot(ah, bh) + (dot(ah, bl) + dot(al, bh))


def onehot_rows(onehot, x):
    high = x.astype(BF16)
    rest = x - high.astype(F32)
    mid = rest.astype(BF16)
    low = (rest - mid.astype(F32)).astype(BF16)
    return (dot(onehot, high) + dot(onehot, mid)) + dot(onehot, low)


def iota(shape, dim):
    return lax.broadcasted_iota(jnp.int32, shape, dim)


def eliminate(a_ref, xl_ref, xu_ref, t_ref, index, half):
    local = pl.multiple_of(index * 16, 16)
    start = pl.multiple_of(half * NB + local, 16)
    sub = iota((16, NB), 0)
    lane = iota((16, NB), 1)
    original = [a_ref[g, pl.ds(start, 16), :] for g in range(2)]
    rolled = pltpu.roll(original[half], lax.rem(NB - local, NB), axis=1)
    cols = [jnp.broadcast_to(rolled[:, j : j + 1], (16, NB)) for j in range(16)]
    upper = list(original[half:])
    jordan = list(original[half:])
    ident = jnp.where((lane == sub) | (lane == sub + 16), 1.0, 0.0).astype(F32)
    factors = jnp.zeros((16, NB), F32)
    scale = jnp.zeros((16, NB), F32)

    def pick(x, k):
        return jnp.broadcast_to(x[k : k + 1, :], (16, NB))

    for k in range(16):
        inverse = 1.0 / pick(cols[k], k)
        mult = cols[k] * inverse
        low = jnp.where(sub > k, mult, 0.0)
        both = jnp.where(sub != k, mult, 0.0)
        for j in range(k + 1, 16):
            cols[j] = cols[j] - both * pick(cols[j], k)
        upper = [x - low * pick(x, k) for x in upper]
        jordan = [x - both * pick(x, k) for x in jordan]
        mixed = jnp.where(lane < 16, low, both - low)
        ident = ident - mixed * pick(ident, k)
        factors = jnp.where((lane == local + k) & (sub > k), mult, factors)
        scale = jnp.where(sub == k, inverse, scale)

    in_block = (lane >= local) & (lane < local + 16)
    lower_of_block = in_block & (lane - local < sub)
    merged = jnp.where(lower_of_block, factors, jnp.where(lane < local, original[half], upper[0]))
    a_ref[half, pl.ds(start, 16), :] = merged
    if half == 0:
        a_ref[1, pl.ds(start, 16), :] = upper[1]
    left_inv = pltpu.roll(jnp.where(lane < 16, ident, 0.0), local, axis=1)
    right_inv = pltpu.roll(
        jnp.where((lane >= 16) & (lane < 32), ident * scale, 0.0), lax.rem(local + NB - 16, NB), axis=1
    )
    zero = jnp.zeros((16, NB), F32)
    xl_ref[half, pl.ds(start, 16), :] = left_inv
    xl_ref[1 - half, pl.ds(start, 16), :] = zero
    xu_ref[half, pl.ds(start, 16), :] = right_inv
    xu_ref[1 - half, pl.ds(start, 16), :] = zero

    t_ref[0, pl.ds(local, 16), :] = jnp.where(
        lane >= local + 16, jordan[0] * scale, jnp.where(in_block, right_inv, 0.0)
    )
    if half == 0:
        t_ref[1, pl.ds(local, 16), :] = jordan[1] * scale
    rows = 2 * NB - half * NB
    below = iota((rows, NB), 0) + half * NB >= start + 16
    wide_lane = iota((rows, NB), 1)
    block_lane = (wide_lane >= local) & (wide_lane < local + 16)
    panel = a_ref[half, half * NB :, :]
    panel_parts = split(panel)
    product = dot3(panel_parts, split(t_ref[0]))
    a_ref[half, half * NB :, :] = jnp.where(
        below, jnp.where(block_lane, product, panel - product), panel
    )
    if half == 0:
        other = a_ref[1]
        product = dot3(panel_parts, split(t_ref[1]))
        a_ref[1] = jnp.where(below, other - product, other)
    t_ref[0, pl.ds(local, 16), :] = zero
    if half == 0:
        t_ref[1, pl.ds(local, 16), :] = zero


def inverses(a_ref, xl_ref, xu_ref):
    packed = jnp.concatenate([a_ref[0], a_ref[1]], 1)
    left = jnp.concatenate([xl_ref[0], xl_ref[1]], 1)
    right = jnp.concatenate([xu_ref[0], xu_ref[1]], 1)
    row = iota((256, 256), 0)
    col = iota((256, 256), 1)
    size = 16
    while size < 256:
        pair = row // (2 * size) == col // (2 * size)
        low_corner = pair & (row % (2 * size) >= size) & (col % (2 * size) < size)
        up_corner = pair & (row % (2 * size) < size) & (col % (2 * size) >= size)
        left_parts = split(left)
        right_parts = split(right)
        first = dot3(left_parts, split(jnp.where(low_corner, packed, 0.0)))
        second = dot3(right_parts, split(jnp.where(up_corner, packed, 0.0)))
        left = left - dot3(split(first), left_parts)
        right = right - dot3(split(second), right_parts)
        size *= 2
    return packed, left, right


def lu_kernel(square_ref, packed_ref, linv_ref, uinv_ref, a_ref, xl_ref, xu_ref, t_ref):
    a_ref[...] = square_ref[...]
    t_ref[...] = jnp.zeros(t_ref.shape, F32)
    for half in range(2):
        def step(index, carry, half=half):
            eliminate(a_ref, xl_ref, xu_ref, t_ref, index, half)
            return carry

        lax.fori_loop(0, 8, step, 0)
    packed, left, right = inverses(a_ref, xl_ref, xu_ref)
    packed_ref[...] = packed
    linv_ref[...] = left
    uinv_ref[...] = right


def lu_call(square):
    result = jax.ShapeDtypeStruct((2 * NB, 2 * NB), F32)
    return pl.pallas_call(
        lu_kernel,
        out_shape=[result] * 3,
        scratch_shapes=[pltpu.VMEM((2, 2 * NB, NB), F32)] * 3 + [pltpu.VMEM((2, NB, NB), F32)],
        compiler_params=pltpu.CompilerParams(vmem_limit_bytes=32 * 2**20),
        name="factor",
    )(square)


def panel_line(number):
    return (number >> 4) * PIECE + NB + (number & 15)


def index_kernel(piv_ref, idx_ref, slot_ref):
    lane = iota((NB, NB), 1).astype(F32)
    sub = iota((NB, NB), 0).astype(F32)

    def rows(x):
        return jnp.broadcast_to(x, (NB, NB))

    def lanes_sum(cond, value=1.0):
        return rows(jnp.sum(jnp.where(cond, value, 0.0), axis=1, keepdims=True))

    def subs_sum(cond, value=1.0):
        return rows(jnp.sum(jnp.where(cond, value, 0.0), axis=0, keepdims=True))

    given = piv_ref[...].astype(F32)
    row = [rows(given[s : s + 1, :]) for s in range(2)]
    col = [x.T for x in row]
    fill_row, fill_col = [], []
    for s in range(2):
        start = float(s * NB)
        listed_row = subs_sum(col[s] == lane + start)
        listed_col = lanes_sum(row[s] == sub + start)
        rank_vacated = lanes_sum((lane <= sub) & (row[s] >= start + NB))
        rank_displaced = subs_sum((sub <= lane) & (listed_col == 0.0))
        pairing = (col[s] >= start + NB) & (listed_row == 0.0) & (rank_vacated == rank_displaced)
        filler = lanes_sum(pairing, lane + start)
        fill_col.append(filler)
        fill_row.append(filler.T)
    again = col[1] == row[0]
    source_col = jnp.where(lanes_sum(again) > 0.0, lanes_sum(again, fill_row[0]), col[1])
    moved = fill_col[1] == row[0]
    second_col = jnp.where(lanes_sum(moved) > 0.0, lanes_sum(moved, fill_row[0]), fill_col[1])

    def whole(x):
        return x.astype(jnp.int32)

    def place(value):
        number = whole(value)
        return (number >> 7) & 3, (number >> 9) * NB + (number & (NB - 1))

    def ranks(keys):
        keys_row = [k.astype(F32) for k in keys]
        keys_col = [k.T for k in keys_row]
        first = subs_sum((keys_col[0] == keys_row[0]) & (sub < lane))
        second = subs_sum((keys_col[1] == keys_row[1]) & (sub < lane)) + subs_sum(
            keys_col[0] == keys_row[1]
        )
        return [whole(first), whole(second)]

    sources = [row[0], source_col.T]
    owners, locals_ = zip(*[place(x) for x in sources])
    rank_arr = ranks(owners)
    slots = [o * SLOTS_A + r for o, r in zip(owners, rank_arr)]
    valid = [(row[0] >= 2.0 * NB) & (subs_sum(again) == 0.0), row[1] >= 2.0 * NB]
    origins = [whole(fill_row[0]), whole(second_col.T)]
    dests, targets = zip(*[place(x) for x in row])
    halves = [x >> 7 for x in origins]
    keys = [jnp.where(v, h * 4 + d, 9) for v, h, d in zip(valid, halves, dests)]
    rank_disp = ranks(keys)
    zero = jnp.zeros((NB, NB), jnp.int32)
    over = zero
    for g in range(2):
        over = over + whole(rows(jnp.sum(jnp.where(rank_arr[g] >= SLOTS_A, 1.0, 0.0), axis=1, keepdims=True)))
        bad = valid[g] & (rank_disp[g] >= SLOTS_D)
        over = over + whole(rows(jnp.sum(jnp.where(bad, 1.0, 0.0), axis=1, keepdims=True)))
    me = lax.axis_index("prow")

    def compact(chosen, values, keys):
        chosen = [jnp.where(c, 1.0, 0.0) for c in chosen]
        chosen_col = [c.T for c in chosen]
        keys_col = [k.T for k in keys]
        before = [
            sum(subs_sum((c > 0.0) & (k < key)) for c, k in zip(chosen_col, keys_col)) for key in keys
        ]
        total = sum(subs_sum(c > 0.0) for c in chosen_col)
        order = [jnp.where(c > 0.0, r, -1.0).T for c, r in zip(chosen, before)]
        packed = []
        for value in values:
            value_col = [v.astype(F32).T for v in value]
            packed.append(
                [
                    whole(sum(subs_sum(o == lane + g * NB, v) for o, v in zip(order, value_col)))
                    for g in range(2)
                ]
            )
        count = whole(total)
        return packed, [count, count]

    (arr_local,), _ = compact([o == me for o in owners], [locals_], [lane, lane + NB])
    out_slot = [
        jnp.where(v & (h == me), d * SLOTS_D + r, -1).astype(F32).T
        for v, h, d, r in zip(valid, halves, dests, rank_disp)
    ]
    out_row = [(x & (NB - 1)).astype(F32).T for x in origins]
    out_local = [
        whole(sum(subs_sum(o == lane + g * NB, v) for o, v in zip(out_slot, out_row))) for g in range(2)
    ]
    (in_target, in_row, in_line, in_origin), in_count = compact(
        [v & (d == me) for v, d in zip(valid, dests)],
        [
            targets,
            [h * NB + r for h, r in zip(halves, rank_disp)],
            [panel_line(h * SLOTS_D + r) for h, r in zip(halves, rank_disp)],
            origins,
        ],
        [t.astype(F32) for t in targets],
    )
    fields = [
        owners, locals_, [over, over], arr_local, out_local,
        in_target, in_row, in_line, in_origin, in_count,
    ]
    for number, field in enumerate(fields):
        for g in range(2):
            idx_ref[number : number + 1, g * NB : (g + 1) * NB] = field[g][0:1, :]
    for number in range(len(fields), 16):
        idx_ref[number : number + 1, :] = jnp.zeros((1, 2 * NB), jnp.int32)
    for g in range(2):
        slot_ref[g * NB : (g + 1) * NB, :] = whole(slots[g].astype(F32).T)


def index_call(pivots):
    return pl.pallas_call(
        index_kernel,
        out_shape=[
            jax.ShapeDtypeStruct((16, 2 * NB), jnp.int32),
            jax.ShapeDtypeStruct((2 * NB, NB), jnp.int32),
        ],
        name="indices",
    )(pivots)


ANY = pl.BlockSpec(memory_space=pl.ANY)


def rows8(start, size):
    return pl.ds(pl.multiple_of(start, 8), size)


def front_kernel(
    idx_ref, slot_ref, x_ref, recv_arr, recv_disp, panel, packed_ref, linv_ref, uinv_ref,
    whole, top, arr_ref, disp_ref, arr_line_ref, disp_line_ref, raw_ref, arr_buf, disp_buf, square,
    a_ref, xl_ref, xu_ref, t_ref,
    load_sem, local_sem, y_send, y_recv, p_send, p_recv, t_send, t_recv, s_send, s_recv,
    scatter_send, scatter_recv, x_send, x_recv, z_send, z_recv, pair_send, pair_recv,
):
    lines = whole.shape[0] // (16 * NB)
    size = whole.shape[0] // LOADS
    load_top = pltpu.make_async_copy(x_ref.at[pl.ds(0, NB * lines)], top, local_sem.at[5])
    load_top.start()
    loads = []
    for number in range(LOADS):
        here = pl.ds(number * size, size)
        loads.append(pltpu.make_async_copy(x_ref.at[here], whole.at[here], load_sem.at[number]))
        loads[-1].start()
    p = lax.axis_index("prow")
    q = lax.axis_index("pcol")
    cx, cz, core = q // 8, (q // 2) % 4, q % 2
    root = q < 2

    def column(ix, iz, icore):
        return (ix % 4 * 4 + iz % 4) * 2 + icore

    up, down, across = ((p + 1) % 4, q), ((p + 3) % 4, q), ((p + 2) % 4, q)
    sibling = (p, column(cx, cz, 1 - core))
    x_peers = [(p, column(cx + i, cz, core)) for i in (1, 2, 3)]
    z_peers = [(p, column(cx, cz + i, core)) for i in (1, 2, 3)]
    near = [up, down, across, sibling] + x_peers + z_peers
    barrier = pltpu.get_barrier_semaphore()
    for other in near:
        pl.semaphore_signal(barrier, inc=1, device_id=other, device_id_type=MESH)

    @pl.when((cx > 0) & (cz > 0))
    def _():
        pl.semaphore_signal(barrier, inc=1, device_id=(p, core), device_id_type=MESH)

    def remote(src, dst, send, recv, device):
        return pltpu.make_async_remote_copy(
            src_ref=src, dst_ref=dst, send_sem=send, recv_sem=recv, device_id=device, device_id_type=MESH
        )

    load_top.wait()

    def displaced(t, carry):
        disp_ref[pl.ds(t * lines, lines), :] = top[pl.ds(idx_ref[OUT_LOCAL, t] * lines, lines), :]
        return carry

    def arriving(j, carry):
        arr_ref[pl.ds(j * lines, lines), :] = whole[pl.ds(idx_ref[ARR_LOCAL, j] * lines, lines), :]
        return carry

    @pl.when(p < 2)
    def _():
        lax.fori_loop(0, 4 * SLOTS_D, displaced, 0, unroll=4)
        disp_line_ref[...] = disp_ref[pl.ds(0, 4 * SLOTS_D, lines), :]

    pl.semaphore_wait(barrier, jnp.where(root, len(near) + 9, len(near)))

    def arr_lines(owner):
        return arr_buf.at[rows8(owner * SLOTS_A, SLOTS_A)]

    def disp_lines(half):
        return disp_buf.at[rows8(half * SLOTS_D, SLOTS_D)]

    def disp_for(owner):
        return disp_line_ref.at[rows8(owner * SLOTS_D, SLOTS_D)]

    peers = [up, down, across]
    own_arr = pltpu.make_async_copy(arr_line_ref, arr_lines(p), local_sem.at[1])
    own_disp = pltpu.make_async_copy(disp_for(p), disp_lines(p % 2), local_sem.at[2])
    arr_panel = [remote(arr_line_ref, arr_lines(p), p_send.at[i], p_recv.at[i], peers[i]) for i in range(3)]
    disp_panel = [
        remote(disp_for(peers[i][0]), disp_lines(p % 2), p_send.at[3 + i], p_recv.at[3 + p % 2], peers[i])
        for i in range(3)
    ]

    @pl.when(root & (p < 2))
    def _():
        for copy in disp_panel:
            copy.start()
        own_disp.start()

    arr_size, disp_size = arr_ref.shape[0], disp_ref.shape[0] // 4
    half_size = arr_size // 2
    low, high = pl.ds(0, half_size), pl.ds(half_size, half_size)

    def arr_rows(owner, part):
        return recv_arr.at[rows8(owner * arr_size + part.start, part.size)]

    def moved_to(owner):
        return disp_ref.at[rows8(owner * disp_size, disp_size)]

    def moved(half):
        return recv_disp.at[rows8(half * (recv_disp.shape[0] // 2), disp_size)]

    own_rows = pltpu.make_async_copy(arr_ref, recv_arr.at[rows8(p * arr_size, arr_size)], local_sem.at[3])
    own_moved = pltpu.make_async_copy(moved_to(p), moved(p % 2), local_sem.at[4])
    bulk = [
        remote(arr_ref.at[low], arr_rows(p, low), y_send.at[0], y_recv.at[0], up),
        remote(arr_ref.at[high], arr_rows(p, high), y_send.at[1], y_recv.at[1], down),
        remote(arr_ref.at[high], arr_rows(p, high), y_send.at[2], y_recv.at[2], up),
        remote(arr_ref.at[low], arr_rows(p, low), y_send.at[3], y_recv.at[3], down),
    ]
    half = p % 2
    to_up = remote(moved_to(up[0]), moved(half), y_send.at[4], y_recv.at[4 + half], up)
    to_down = remote(moved_to(down[0]), moved(half), y_send.at[5], y_recv.at[4 + half], down)
    to_across = remote(moved_to(across[0]), moved(half), y_send.at[6], y_recv.at[4 + half], across)

    @pl.when(p < 2)
    def _():
        to_across.start()
        own_moved.start()

    forward = [
        remote(arr_rows(down[0], low), arr_rows(down[0], low), y_send.at[7], y_recv.at[7], up),
        remote(arr_rows(up[0], high), arr_rows(up[0], high), y_send.at[8], y_recv.at[8], down),
    ]
    for load in loads:
        load.wait()
    lax.fori_loop(0, SLOTS_A, arriving, 0, unroll=4)
    arr_line_ref[...] = arr_ref[pl.ds(0, SLOTS_A, lines), :]

    @pl.when(root)
    def _():
        for copy in arr_panel:
            copy.start()
        own_arr.start()

    for copy in bulk:
        copy.start()
    own_rows.start()

    @pl.when(p < 2)
    def _():
        to_up.start()
        to_down.start()

    upper, lower = square.at[core, pl.ds(0, NB)], square.at[core, pl.ds(NB, NB)]
    upper_x = [remote(upper, upper, t_send.at[0, i], t_recv.at[0], x_peers[i]) for i in range(3)]
    lower_z = [remote(lower, lower, t_send.at[1, i], t_recv.at[1], z_peers[i]) for i in range(3)]
    upper_z = [remote(upper, upper, t_send.at[2, i], t_recv.at[0], z_peers[i]) for i in range(3)]
    lower_x = [remote(lower, lower, t_send.at[3, i], t_recv.at[1], x_peers[i]) for i in range(3)]
    own_square = remote(square.at[core], square.at[core], s_send.at[0], s_recv.at[0], sibling)

    start, end = pl.ds(0, PIECE // 2), pl.ds(PIECE // 2, PIECE // 2)
    scatter = [
        remote(
            raw_ref.at[i], panel.at[core, i // 4, i % 4, pl.ds(0, NB)], scatter_send.at[i - 1], scatter_recv.at[0],
            (p, column(i // 4, i % 4, core)),
        )
        for i in range(1, 16)
    ]
    scatter_lines = [
        remote(
            disp_buf.at[pl.ds(16 * i, 16)], panel.at[core, i // 4, i % 4, pl.ds(NB, 16)],
            scatter_send.at[14 + i], scatter_recv.at[1], (p, column(i // 4, i % 4, core)),
        )
        for i in range(1, 16)
    ]
    own_piece = pltpu.make_async_copy(raw_ref.at[0], panel.at[core, 0, 0, pl.ds(0, NB)], local_sem.at[0])
    own_lines = pltpu.make_async_copy(
        disp_buf.at[pl.ds(0, 16)], panel.at[core, 0, 0, pl.ds(NB, 16)], local_sem.at[6]
    )
    along = []
    for i in range(3):
        mine_low, mine_high = panel.at[core, cx, cz, start], panel.at[core, cx, cz, end]
        along.append(remote(mine_low, mine_low, x_send.at[0, i], x_recv.at[0, i], x_peers[i]))
        along.append(remote(mine_high, mine_high, z_send.at[0, i], z_recv.at[0, i], z_peers[i]))
    spread = []
    for i in range(3):
        mine_low, mine_high = panel.at[core, :, cz, start], panel.at[core, cx, :, end]
        spread.append(remote(mine_low, mine_low, z_send.at[1, i], z_recv.at[1, i], z_peers[i]))
        spread.append(remote(mine_high, mine_high, x_send.at[1, i], x_recv.at[1, i], x_peers[i]))
    pair = remote(panel.at[core], panel.at[core], pair_send.at[0], pair_recv.at[0], sibling)

    @pl.when(root)
    def _():
        for i in range(16):
            raw_ref[i] = whole[pl.ds(i * NB * lines, NB, lines), :]
        for copy in scatter:
            copy.start()
        own_piece.start()
        disp_buf[pl.ds(2 * SLOTS_D, 2 * NB - 2 * SLOTS_D), :] = jnp.zeros((2 * NB - 2 * SLOTS_D, NB), F32)
        own_arr.wait()
        for copy in arr_panel:
            copy.wait_recv()
        onehot = jnp.where(iota((2 * NB, 4 * SLOTS_A), 1) == slot_ref[:, :1], 1.0, 0.0).astype(BF16)
        square[core] = onehot_rows(onehot, arr_buf[...])
        for copy in upper_x + lower_z:
            copy.start()

    @pl.when(jnp.logical_not(root))
    def _():
        upper_x[0].wait_recv()

    @pl.when(cz == 0)
    def _():
        for copy in upper_z:
            copy.start()

    @pl.when(jnp.logical_not(root))
    def _():
        lower_z[0].wait_recv()

    @pl.when(cx == 0)
    def _():
        for copy in lower_x:
            copy.start()

    own_square.start()

    @pl.when(root)
    def _():
        for source in range(2):
            @pl.when(p == source)
            def _():
                own_disp.wait()

            @pl.when(p != source)
            def _(source=source):
                remote(disp_for(0), disp_lines(source), p_send.at[3], p_recv.at[3 + source], up).wait_recv()
        for copy in scatter_lines:
            copy.start()
        own_lines.start()

    own_square.wait_recv()
    a_ref[...] = square[...]
    t_ref[...] = jnp.zeros(t_ref.shape, F32)

    def pass_rows():
        bulk[0].wait_recv()
        forward[0].start()
        bulk[1].wait_recv()
        forward[1].start()

    def pass_piece():
        @pl.when(root)
        def _():
            own_piece.wait()
            own_lines.wait()

        @pl.when(jnp.logical_not(root))
        def _():
            scatter[0].wait_recv()
            scatter_lines[0].wait_recv()

        for copy in along:
            copy.start()

    def pass_pieces():
        for copy in along:
            copy.wait_recv()
        for copy in spread:
            copy.start()

    def pass_panel():
        for copy in spread:
            copy.wait_recv()
        pair.start()

    events = [{3: pass_piece, 5: pass_rows}, {0: pass_pieces, 7: pass_panel}]
    for half_number in range(2):
        def factor_step(index, carry, half_number=half_number):
            for when, event in events[half_number].items():
                pl.when(index == when)(event)
            eliminate(a_ref, xl_ref, xu_ref, t_ref, index, half_number)
            return carry

        lax.fori_loop(0, 8, factor_step, 0)
    packed, left, right = inverses(a_ref, xl_ref, xu_ref)
    packed_ref[...] = packed
    linv_ref[...] = left
    uinv_ref[...] = right

    bulk[2].wait_recv()
    bulk[3].wait_recv()
    for copy in forward:
        copy.wait_recv()
    own_rows.wait()
    for source in range(2):
        @pl.when(p == source)
        def _():
            own_moved.wait()

        @pl.when(p != source)
        def _(source=source):
            remote(moved_to(0), moved(source), y_send.at[4], y_recv.at[4 + source], up).wait_recv()
    pair.wait_recv()
    for copy in bulk + forward + along + spread + [pair]:
        copy.wait_send()

    @pl.when(p < 2)
    def _():
        to_up.wait_send()
        to_down.wait_send()
        to_across.wait_send()

    @pl.when(cz == 0)
    def _():
        for copy in upper_z:
            copy.wait_send()

    @pl.when(cx == 0)
    def _():
        for copy in lower_x:
            copy.wait_send()

    own_square.wait_send()

    @pl.when(root)
    def _():
        for copy in arr_panel + upper_x + lower_z + scatter + scatter_lines:
            copy.wait_send()

        @pl.when(p < 2)
        def _():
            for copy in disp_panel:
                copy.wait_send()


def front_call(idx, slot, x, lines):
    dma = pltpu.SemaphoreType.DMA
    vmem = pl.BlockSpec(memory_space=pltpu.VMEM)
    result = jax.ShapeDtypeStruct((2 * NB, 2 * NB), F32)
    sizes = [(4 * SLOTS_A * lines,), (2 * NB * lines,), (2, 4, 4, PIECE)]
    held = [
        x.shape[:1], (NB * lines,), (SLOTS_A * lines,), (4 * SLOTS_D * lines,), (SLOTS_A,), (4 * SLOTS_D,), (16, NB),
        (4 * SLOTS_A,), (2 * NB,), (2, 2 * NB), (2, 2 * NB), (2, 2 * NB), (2, 2 * NB), (2, NB),
    ]
    semaphores = [
        (LOADS,), (7,), (9,), (9,), (6,), (5,), (4, 3), (2,), (1,), (1,),
        (30,), (2,), (2, 3), (2, 3), (2, 3), (2, 3), (1,), (1,),
    ]
    return pl.pallas_call(
        front_kernel,
        in_specs=[pl.BlockSpec(memory_space=pltpu.SMEM), vmem, ANY],
        out_specs=[ANY] * 3 + [vmem] * 3,
        out_shape=[jax.ShapeDtypeStruct(size + (NB,), F32) for size in sizes] + [result] * 3,
        scratch_shapes=[pltpu.VMEM(size + (NB,), F32) for size in held] + [dma(shape) for shape in semaphores],
        compiler_params=pltpu.CompilerParams(
            collective_id=0, has_side_effects=True, vmem_limit_bytes=48 * 2**20
        ),
        name="front",
    )(idx, slot, x)


STEP_ROWS = 512
AHEAD = 2


def update_kernel(
    idx_ref, x_ref, panel_ref, disp_in, arr_in, slot_ref, packed_ref, linv_ref, uinv_ref, o_ref,
    whole, pan, disp_ref, arr_ref, stacked, u_ref, done, x_sem, pan_sem, disp_sem, arr_sem,
):
    p = lax.axis_index("prow")
    q = lax.axis_index("pcol")
    step = pl.program_id(0)
    lines = whole.shape[0] // (16 * NB)
    size = STEP_ROWS * lines

    def load_x(number):
        here = pl.ds(pl.multiple_of(number * size, 8), size)
        return pltpu.make_async_copy(x_ref.at[here], whole.at[here], x_sem.at[number])

    @pl.when(step == 0)
    def _():
        loads = []
        part = 4 * SLOTS_A * lines // 4
        for number in range(4):
            here = pl.ds(number * part, part)
            loads.append(pltpu.make_async_copy(arr_in.at[here], arr_ref.at[here], arr_sem.at[number]))
        for half in range(2):
            loads.append(pltpu.make_async_copy(panel_ref.at[half], pan.at[half], pan_sem.at[half]))
            here = pl.ds(half * NB * lines, NB * lines)
            loads.append(pltpu.make_async_copy(disp_in.at[here], disp_ref.at[here], disp_sem.at[half]))
        for load in loads:
            load.start()
        load_x(0).start()
        done[0] = 0
        high, low = split(linv_ref[...])
        slot = slot_ref[:, :1]
        onehot = jnp.where(iota((2 * NB, 4 * SLOTS_A), 1) == slot, 1.0, 0.0).astype(BF16)
        left = (dot(high, onehot).astype(BF16), dot(low, onehot).astype(BF16))
        for load in loads[:4]:
            load.wait()
        for number in range(1, AHEAD):
            load_x(number).start()
        for c in range(lines):
            rows = arr_ref[pl.ds(c, 4 * SLOTS_A, lines), :]
            value = dot3(left, split(rows))
            here = slice(c * NB, (c + 1) * NB)
            u_ref[:, here] = value
            upper, rest = split(value)
            stacked[0 : 2 * NB, here] = upper
            stacked[2 * NB : 4 * NB, here] = rest
            stacked[4 * NB : 6 * NB, here] = upper
        for load in loads[4:]:
            load.wait()

    @pl.when(step + AHEAD < 16 * NB // STEP_ROWS)
    def _():
        load_x(step + AHEAD).start()

    load_x(step).wait()
    bound = (step + 1) * STEP_ROWS

    def more(t):
        return (t < idx_ref[IN_COUNT, 0]) & (idx_ref[IN_TARGET, jnp.minimum(t, 2 * NB - 1)] < bound)

    def patch(t):
        target = idx_ref[IN_TARGET, t]
        line = idx_ref[IN_LINE, t]
        panel_row = (target >> 7) * PIECE + (target & (NB - 1))
        for half in range(2):
            pan[half, pl.ds(panel_row, 1), :] = pan[half, pl.ds(line, 1), :]
        source = idx_ref[IN_ROW, t] * lines
        whole[pl.ds(target * lines, lines), :] = disp_ref[pl.ds(source, lines), :]
        return t + 1

    done[0] = lax.while_loop(more, patch, done[0])

    rows = []
    for number in range(STEP_ROWS // NB):
        here = pl.ds(pl.multiple_of((step * (STEP_ROWS // NB) + number) * PIECE, 8), NB)
        rows.append(jnp.concatenate([pan[0, here, :], pan[1, here, :]], 1))
    rows = jnp.concatenate(rows, 0)
    mult = dot3(split(rows), split(uinv_ref[...]))
    high, low = split(mult)
    left = jnp.concatenate([high, high, low], 1)
    base = step * (STEP_ROWS * lines)
    for c in range(0, lines, 2):
        product = dot(left, stacked[:, c * NB : (c + 2) * NB])
        for k in range(2):
            current = whole[pl.ds(base + c + k, STEP_ROWS, lines), :]
            o_ref[pl.ds(c + k, STEP_ROWS, lines), :] = current - product[:, k * NB : (k + 1) * NB]

    for half in range(2):
        @pl.when(q == half)
        def _(half=half):
            o_ref[pl.ds(0, STEP_ROWS, lines), :] = mult[:, half * NB : (half + 1) * NB]

    for half in range(2):
        @pl.when((p == half) & (step == 0))
        def _(half=half):
            top = slice(half * NB, (half + 1) * NB)
            for c in range(lines):
                value = u_ref[top, c * NB : (c + 1) * NB]
                if c == 0:
                    value = jnp.where(q == 0, packed_ref[top, :NB], jnp.where(q == 1, packed_ref[top, NB:], value))
                o_ref[pl.ds(c, NB, lines), :] = value


def update_call(idx, x, panel, disp, arr, slot, packed, linv, uinv, lines):
    vmem = pl.BlockSpec(memory_space=pltpu.VMEM)
    return pl.pallas_call(
        update_kernel,
        grid=(16 * NB // STEP_ROWS,),
        in_specs=[pl.BlockSpec(memory_space=pltpu.SMEM)] + [ANY] * 4 + [vmem] * 4,
        out_specs=pl.BlockSpec((STEP_ROWS * lines, NB), lambda i: (i, 0)),
        out_shape=jax.ShapeDtypeStruct((16 * NB * lines, NB), F32),
        scratch_shapes=[
            pltpu.VMEM((16 * NB * lines, NB), F32),
            pltpu.VMEM((2, 16 * PIECE, NB), F32),
            pltpu.VMEM((2 * NB * lines, NB), F32),
            pltpu.VMEM((4 * SLOTS_A * lines, NB), F32),
            pltpu.VMEM((6 * NB, NB * lines), BF16),
            pltpu.VMEM((2 * NB, NB * lines), F32),
            pltpu.SMEM((1,), jnp.int32),
            pltpu.SemaphoreType.DMA((16 * NB // STEP_ROWS,)),
            pltpu.SemaphoreType.DMA((2,)),
            pltpu.SemaphoreType.DMA((2,)),
            pltpu.SemaphoreType.DMA((4,)),
        ],
        compiler_params=pltpu.CompilerParams(vmem_limit_bytes=48 * 2**20),
        name="update",
    )(idx, x, panel, disp, arr, slot, packed, linv, uinv)


def shards(matrix, pivots):
    lines = matrix.shape[3]
    rows = matrix.shape[0] * NB
    p = lax.axis_index("prow")
    q = lax.axis_index("pcol")
    x = matrix.reshape(rows * lines, NB)
    idx, slot = index_call(pivots)

    def total(x, axis, count):
        bit = 1
        while bit < count:
            x = x + lax.ppermute(x, axis, [(i, i ^ bit) for i in range(count)])
            bit *= 2
        return x

    def fits(x, idx, slot):
        recv_arr, recv_disp, panel, packed, linv, uinv = front_call(idx, slot, x, lines)
        return recv_arr, recv_disp, panel, packed, linv, uinv, idx, slot

    def general(x, idx, slot):
        x = x.reshape(rows, lines, NB)
        chosen = jnp.where((idx[OWNER] == p)[:, None, None], jnp.take(x, idx[LOCAL], axis=0), 0.0)
        top = jnp.concatenate([jnp.where(p == s, x[:NB], 0.0) for s in range(2)])
        chosen, top = total(chosen, "prow", 4), total(top, "prow", 4)
        own = jnp.concatenate([x[:, 0].reshape(16, NB, NB), top[:, 0].reshape(16, 16, NB)], 1)
        own = jnp.concatenate([own.reshape(-1, NB), chosen[:, 0]])
        both = total(jnp.stack([jnp.where(q == s, own, 0.0) for s in range(2)]), "pcol", 32)
        panel = both[:, : 16 * PIECE].reshape(2, 4, 4, PIECE, NB)
        order = jnp.arange(2 * NB, dtype=jnp.int32)
        idx = idx.at[IN_ROW].set(idx[IN_ORIGIN]).at[IN_LINE].set(panel_line(idx[IN_ORIGIN]))
        slot = jnp.broadcast_to(order[:, None], slot.shape)
        packed, linv, uinv = lu_call(both[:, 16 * PIECE :])
        chosen = jnp.pad(chosen, ((0, 4 * SLOTS_A - 2 * NB), (0, 0), (0, 0)))
        return chosen.reshape(-1, NB), top.reshape(-1, NB), panel, packed, linv, uinv, idx, slot

    arr, disp, panel, packed, linv, uinv, idx, slot = lax.cond(idx[OVER, 0] == 0, fits, general, x, idx, slot)
    panel = panel.reshape(2, -1, NB)
    out = update_call(idx, x, panel, disp, arr, slot, packed, linv, uinv, lines)
    return out.reshape(matrix.shape)


def solution(mesh):
    placed = (P(None, "prow", None, None, "pcol", None), P())
    return jax.shard_map(
        shards,
        mesh=mesh,
        in_specs=placed,
        out_specs=P(None, "prow", None, None, "pcol", None),
        check_vma=False,
    )
```
